32 devices in a mesh: section: 4 (over z), dp: 4 (over y, x), head: 2 (over core).
Axes of the slice: x: 2, y: 2, z: 4, core: 2. Of those that a mesh axis runs over, the one named last changes fastest.
Arguments:
- segments: int32 [5, 512], P(None, 'dp'), may hold values from 0 to 15, never falling along the last dimension, each value on 1 to 64 neighbouring positions
- section_input_stream: bfloat16 [4, 512, 2048], P('section', 'dp', 'head'), may hold values from -16 to 16
- entering: bfloat16 [512, 2048], P('dp'), may hold values from -16 to 16
- pending_first_values: bfloat16 [4, 512, 512], P('section', 'dp', 'head'), may hold values from -6 to 6
- norm_gain_vector: float32 [4, 2048], P('section'), may hold values from 0.1 to 1.9
- query_weight: bfloat16 [4, 2048, 2048], P('section', None, 'head'), may hold values from -0.110485435 to 0.110485435
- key_weight: bfloat16 [4, 2048, 512], P('section', None, 'head'), may hold values from -0.110485435 to 0.110485435
- value_weight: bfloat16 [4, 2048, 512], P('section', None, 'head'), may hold values from -0.125 to 0.125
- output_weight: bfloat16 [4, 2048, 2048], P('section', None, 'head'), may hold values from -0.125 to 0.125
- query_key_scale: float32 [4, 16], P('section', 'head'), may hold values from 0.7 to 24
- value_blend_weight: float32 [4, 4], P('section', 'head'), may hold values from 0.3 to 1.5
- value_cotangent_rows: bfloat16 [4, 2, 512, 512], P('section', None, 'dp', 'head'), may hold values from -0.125 to 0.125
Outputs:
- first_round: bfloat16 [4, 512, 2048], P('section', 'dp', 'head')
- second_round: bfloat16 [4, 512, 2048], P('section', 'dp', 'head')
- value_weight_grads: float32 [4, 2048, 512], P('section', 'dp', 'head')
The draws below stay inside these ranges and needn't reach their ends.
Inputs may be any that keep to these rules, and one draw needn't show every extreme that they name: `segments`: along each row document ids never fall, and a document holds at most half of 128 tokens.
All inputs are finite; a program needn't handle non-finite values.
Results may differ from the reference program's by a relative error of at most 0.018.
Values may be sent and summed in bfloat16 or wider, within the bound.
A program may use at most 64 MiB of HBM per device.

```python
import math
import jax
import jax.numpy as jnp
import numpy as np
from jax import lax

D = 2048
HEADS = 16
KEY_VALUE_HEADS = 4
HEAD_WIDTH = 128
MB_TOK = 128
ROUNDS = 2
LAYER_COUNT = 4
TOKEN_COUNT = 512
N_DP = 4


def stream_draw(key, array_shape):
    key_base = jax.random.fold_in(key, 0)
    values = jax.random.normal(key_base, array_shape, jnp.float32)
    return jnp.clip(values, -16.0, 16.0)


def draw_section_input_stream(key, part):
    return stream_draw(jax.random.fold_in(key, 3), (LAYER_COUNT, TOKEN_COUNT, D)).astype(jnp.bfloat16)


def draw_entering(key, part):
    return stream_draw(jax.random.fold_in(key, 5), (TOKEN_COUNT, D)).astype(jnp.bfloat16)


def query_key_pair(key):
    key_first, key_second = jax.random.split(jax.random.fold_in(key, 11))
    bound_value = 5.0 * D ** (-0.5)
    key_weights = jax.random.normal(key_first, (LAYER_COUNT, D, KEY_VALUE_HEADS * HEAD_WIDTH), jnp.float32) * D ** (-0.5)
    fresh_draw = jax.random.normal(key_second, (LAYER_COUNT, D, HEADS * HEAD_WIDTH), jnp.float32) * D ** (-0.5)
    query_weights = fresh_draw
    return (jnp.clip(query_weights, -bound_value, bound_value), jnp.clip(key_weights, -bound_value, bound_value))


def draw_query_weight(key, part):
    return query_key_pair(key)[0].astype(jnp.bfloat16)


def draw_key_weight(key, part):
    return query_key_pair(key)[1].astype(jnp.bfloat16)


def draw_query_key_scale(key, part):
    key_base = jax.random.fold_in(jax.random.fold_in(key, 17), 0)
    return jnp.exp(jax.random.uniform(key_base, (LAYER_COUNT, HEADS), jnp.float32, math.log(0.7), math.log(3.0)))


def block_levels(stream_key, extent, shards, least, high):
    def one(dim, blocks):
        heights = jax.random.uniform(jax.random.fold_in(jax.random.fold_in(stream_key, 6), dim), (blocks,), jnp.float32, least / len(shards), high / len(shards))
        return jnp.repeat(jnp.exp(heights), extent[dim] // blocks).reshape((-1,) + (1,) * (len(extent) - dim - 1))

    loudness = one(*shards[0])
    for cut in shards[1:]:
        loudness = loudness * one(*cut)
    return loudness


def split_up(amount, total, most, lean):
    weights = [(1 << 20) // math.isqrt(rank ** lean) + 1 for rank in range(2, amount + 1)]
    spare, given = total - most - (amount - 1), [1] * (amount - 1)
    while spare > 0:
        movable = [i for i in range(amount - 1) if given[i] < most]
        pool, left = sum([weights[i] for i in movable]), spare
        for i in movable:
            extra = min(most - given[i], max(1, left * weights[i] // pool), spare)
            given[i] = given[i] + extra
            spare = spare - extra
    return np.array([most] + given)


def ragged(rng, amount, total, reach, slope):
    if amount == 2:
        one = jax.random.randint(rng, (), max(1, total - reach), min(reach, total - 1) + 1)
        return jnp.stack([one, total - one])
    lengths = jnp.asarray(split_up(amount, total, reach, slope), jnp.int32)
    pairs = (amount - 1) // 2
    donor, receiver = lengths[1:1 + 2 * pairs:2], lengths[2:2 + 2 * pairs:2]
    margin = jnp.minimum(donor - 1, reach - receiver)
    passed = jax.random.randint(jax.random.fold_in(rng, 1), (pairs,), 0, 1 << 20) % (margin + 1)
    lengths = lengths.at[1:1 + 2 * pairs:2].set(donor - passed).at[2:2 + 2 * pairs:2].set(receiver + passed)
    return lengths[jax.random.permutation(jax.random.fold_in(rng, 2), amount)]


def bell_draw(key, extent, spread, bound, cuts=(), kind=jnp.bfloat16):
    entries = jax.random.normal(key, extent, jnp.float32) * spread
    if len(cuts) > 0:
        entries = block_levels(key, extent, cuts, -0.22, 0.18) * entries
    return jnp.clip(entries, min=-bound, max=bound).astype(kind)


def setup_inputs(seed: int = 0) -> dict:
    key_list = jax.random.split(jax.random.key(seed), 13)
    return {
        "segments": jax.vmap(lambda own: jnp.searchsorted(jnp.cumsum(ragged(own, 4 * N_DP, TOKEN_COUNT, MB_TOK // 2, 1)), jnp.arange(TOKEN_COUNT), side="right"))(jax.random.split(key_list[0], (LAYER_COUNT + 1))).reshape((LAYER_COUNT + 1, TOKEN_COUNT)).astype(jnp.int32),
        "section_input_stream": draw_section_input_stream(jax.random.fold_in(key_list[12], 71), 0),
        "entering": draw_entering(jax.random.fold_in(key_list[12], 71), 0),
        "pending_first_values": bell_draw(key_list[3], (LAYER_COUNT, TOKEN_COUNT, KEY_VALUE_HEADS * HEAD_WIDTH), 1.0, 6.0, ((0, 4), (1, 4), (2, 2))),
        "norm_gain_vector": jnp.clip(1.0 + 0.18 * jax.random.normal(key_list[4], (LAYER_COUNT, D), jnp.float32), 0.1, 1.9),
        "query_weight": draw_query_weight(jax.random.fold_in(key_list[12], 71), 0),
        "key_weight": draw_key_weight(jax.random.fold_in(key_list[12], 71), 0),
        "value_weight": bell_draw(key_list[7], (LAYER_COUNT, D, KEY_VALUE_HEADS * HEAD_WIDTH), D ** -0.5, 0.125, ((0, 4), (2, 2))),
        "output_weight": bell_draw(key_list[8], (LAYER_COUNT, HEADS * HEAD_WIDTH, D), (HEADS * HEAD_WIDTH) ** -0.5, 0.125, ((0, 4), (2, 2))),
        "query_key_scale": draw_query_key_scale(jax.random.fold_in(key_list[12], 71), 0),
        "value_blend_weight": jnp.clip(jnp.exp(math.log(1.5) - 1.60943787 * jax.random.uniform(key_list[10], (LAYER_COUNT, KEY_VALUE_HEADS), jnp.float32) ** block_levels(key_list[10], (LAYER_COUNT, KEY_VALUE_HEADS), ((0, 4), (1, 2)), -0.2, 0.2)), 0.3, 1.5),
        "value_cotangent_rows": bell_draw(key_list[11], (LAYER_COUNT, ROUNDS, TOKEN_COUNT, KEY_VALUE_HEADS * HEAD_WIDTH), 0.02, 0.125, ((0, 4), (2, 4), (3, 2))),
    }


epsilon = 1e-06

def rms_rows(values):
    return values * lax.rsqrt(lax.optimization_barrier(jnp.mean(values * values, axis=-1, keepdims=True)) + epsilon)

def block_layer(stream, segment_row, feature_gain, query_proj, key_proj, value_proj, out_proj, scales, mixing, earlier_values):
    tokens = stream.shape[0]
    stream_float = stream.astype(jnp.float32)
    normed = (rms_rows(stream_float) * feature_gain).astype(jnp.bfloat16)
    queries = jnp.dot(normed, query_proj, preferred_element_type=jnp.float32).reshape(tokens, HEADS, HEAD_WIDTH)
    key_rows = jnp.dot(normed, key_proj, preferred_element_type=jnp.float32).reshape(tokens, KEY_VALUE_HEADS, HEAD_WIDTH)
    values = jnp.dot(normed, value_proj, preferred_element_type=jnp.float32).reshape(tokens, KEY_VALUE_HEADS, HEAD_WIDTH)
    queries = rms_rows(queries)
    key_rows = rms_rows(key_rows)
    if earlier_values is None:
        mixed_values = values.astype(jnp.bfloat16)
        carried = mixed_values
    else:
        carried = earlier_values.reshape(tokens, KEY_VALUE_HEADS, HEAD_WIDTH)
        mixed_values = (values + mixing[None, :, None] * carried.astype(jnp.float32)).astype(jnp.bfloat16)
    group_size = HEADS // KEY_VALUE_HEADS
    queries = queries.reshape(N_DP, MB_TOK, KEY_VALUE_HEADS, group_size, HEAD_WIDTH)
    key_rows = key_rows.reshape(N_DP, MB_TOK, KEY_VALUE_HEADS, HEAD_WIDTH)
    mixed_blocks = mixed_values.reshape(N_DP, MB_TOK, KEY_VALUE_HEADS, HEAD_WIDTH)
    factor = (scales / math.sqrt(HEAD_WIDTH)).reshape(KEY_VALUE_HEADS, group_size)
    scores = jnp.einsum('nqkgd,ntkd->nkgqt', queries, key_rows) * factor[None, :, :, None, None]
    segment_blocks = segment_row.reshape(N_DP, MB_TOK)
    positions = jnp.arange(MB_TOK)
    allowed = (positions[:, None] >= positions[None, :])[None] & (segment_blocks[:, :, None] == segment_blocks[:, None, :])
    scores = jnp.where(allowed[:, None, None], scores, -jnp.inf)
    row_max = lax.optimization_barrier(jnp.max(scores, axis=-1, keepdims=True))
    exponent = jnp.exp(scores - row_max)
    weights = (exponent / lax.optimization_barrier(jnp.sum(exponent, axis=-1, keepdims=True))).astype(jnp.bfloat16)
    attended = jnp.einsum('nkgqt,ntkd->nqkgd', weights.astype(jnp.float32), mixed_blocks.astype(jnp.float32))
    attended = attended.astype(jnp.bfloat16).reshape(tokens, HEADS * HEAD_WIDTH)
    result = (stream_float + jnp.dot(attended, out_proj, preferred_element_type=jnp.float32)).astype(jnp.bfloat16)
    return (result, normed, carried.reshape(tokens, KEY_VALUE_HEADS * HEAD_WIDTH))

def reference(segments, section_input_stream, entering, pending_first_values, norm_gain_vector, query_weight, key_weight, value_weight, output_weight, query_key_scale, value_blend_weight, value_cotangent_rows):
    first_outputs = []
    first_normed = []
    first_carried = []
    for current_layer_index in range(LAYER_COUNT):
        earlier_values = None if current_layer_index == 0 else pending_first_values[current_layer_index]
        result, normed, carried = block_layer(section_input_stream[current_layer_index], segments[current_layer_index], norm_gain_vector[current_layer_index], query_weight[current_layer_index], key_weight[current_layer_index], value_weight[current_layer_index], output_weight[current_layer_index], query_key_scale[current_layer_index], value_blend_weight[current_layer_index], earlier_values)
        first_outputs.append(result)
        first_normed.append(normed)
        first_carried.append(carried)
    second_outputs = []
    gradients = []
    for current_layer_index in range(LAYER_COUNT):
        if current_layer_index == 0:
            stream = entering
            earlier_values = None
            segment_row = segments[LAYER_COUNT]
        else:
            stream = first_outputs[current_layer_index - 1]
            earlier_values = first_carried[current_layer_index - 1]
            segment_row = segments[current_layer_index - 1]
        result, normed, carried = block_layer(stream, segment_row, norm_gain_vector[current_layer_index], query_weight[current_layer_index], key_weight[current_layer_index], value_weight[current_layer_index], output_weight[current_layer_index], query_key_scale[current_layer_index], value_blend_weight[current_layer_index], earlier_values)
        second_outputs.append(result)
        gradient = jnp.dot(first_normed[current_layer_index].T, value_cotangent_rows[current_layer_index, 0], preferred_element_type=jnp.float32)
        gradient = gradient + jnp.dot(normed.T, value_cotangent_rows[current_layer_index, 1], preferred_element_type=jnp.float32)
        gradients.append(gradient)
    return (jnp.stack(first_outputs), jnp.stack(second_outputs), jnp.stack(gradients))
```

```python
import functools
import math

import jax
import jax.numpy as jnp
from jax import lax
from jax.experimental import pallas as pl
from jax.experimental.pallas import tpu as pltpu
from jax.sharding import PartitionSpec as P

HEAD_WIDTH = 128
CHUNK = 256
EPSILON = 1e-06
F32 = jnp.float32
BF16 = jnp.bfloat16


def rms_rows(values):
    return values * lax.rsqrt(jnp.mean(values * values, axis=-1, keepdims=True) + EPSILON)


def dot(a, b):
    return jnp.dot(a, b, preferred_element_type=F32)


def split_high_low(values):
    high = values.astype(BF16)
    return high, (values - high.astype(F32)).astype(BF16)


def kernel(
    sections,
    replicas,
    heads,
    seg_hbm,
    x_hbm,
    entering_hbm,
    pending_hbm,
    gain_hbm,
    wq_hbm,
    wk_hbm,
    wv_hbm,
    wo_hbm,
    scale_hbm,
    blend_hbm,
    cot_hbm,
    out1_hbm,
    out2_hbm,
    grad_hbm,
    seg,
    gain,
    scale,
    blend,
    wq,
    wk,
    wv,
    wo,
    x1,
    x2,
    f1,
    f2,
    normed1,
    normed2,
    acc,
    att1,
    att2,
    out1,
    out2,
    proj,
    rows_n,
    rows_c,
    grad,
    local_sem,
    weight_sem,
    enter_sem,
    out_sem,
    x_send,
    x_recv,
    c_send,
    c_recv,
    n_send,
    n_recv,
    a_send,
    a_recv,
    z_send,
    z_recv,
    f_send,
    f_recv,
    v_send,
    v_recv,
):
    section = lax.axis_index("section")
    replica = lax.axis_index("dp")
    me = lax.axis_index("head")
    tokens, width = x1.shape[1], x1.shape[2]
    model = width * heads
    q_width, kv_width = wq.shape[1], wk.shape[1]
    kv_heads = kv_width // HEAD_WIDTH
    group = q_width // kv_width
    grad_rows = model // replicas
    chunks = width // CHUNK
    is_first = section == 0
    not_first = section > 0
    not_last = section < sections - 1

    def local(src, dst, sem):
        copy = pltpu.make_async_copy(src, dst, sem)
        copy.start()
        return copy

    def remote(src, dst, send, recv, where):
        return pltpu.make_async_remote_copy(
            src_ref=src,
            dst_ref=dst,
            send_sem=send,
            recv_sem=recv,
            device_id=where,
            device_id_type=pl.DeviceIdType.MESH,
        )

    def head_at(step):
        return lax.rem(me + step, heads)

    def replica_at(step):
        return lax.rem(replica + step, replicas)

    x_load = local(x_hbm.at[0], x1.at[me], local_sem.at[0])
    gain_load = local(gain_hbm, gain, local_sem.at[1])
    wk_load = local(wk_hbm.at[0], wk, weight_sem.at[0])
    wv_load = local(wv_hbm.at[0], wv, weight_sem.at[1])
    quarter = model // 4
    wq_loads = [
        local(
            wq_hbm.at[0, pl.ds(i * quarter, quarter)],
            wq.at[pl.ds(i * quarter, quarter)],
            weight_sem.at[2 + i],
        )
        for i in range(4)
    ]
    seg_load = local(seg_hbm, seg, local_sem.at[2])
    scale_load = local(scale_hbm, scale, local_sem.at[3])
    blend_load = local(blend_hbm, blend, local_sem.at[4])
    cot_load = local(cot_hbm.at[0], rows_c.at[replica], local_sem.at[5])
    f1_load = pltpu.make_async_copy(pending_hbm.at[0], f1, local_sem.at[6])

    @pl.when(not_first)
    def _():
        f1_load.start()

    wo_loads = [
        local(
            wo_hbm.at[0, pl.ds(i * quarter, quarter)],
            wo.at[pl.ds(i * quarter, quarter)],
            weight_sem.at[6 + i],
        )
        for i in range(4)
    ]
    enter_loads = [
        pltpu.make_async_copy(
            entering_hbm.at[:, pl.ds(h * width, width)], x2.at[h], enter_sem.at[h]
        )
        for h in range(heads)
    ]

    @pl.when(is_first)
    def _():
        for load in enter_loads:
            load.start()
        f2[...] = jnp.zeros_like(f2)

    barrier = pltpu.get_barrier_semaphore()

    def greet(where):
        pl.semaphore_signal(barrier, inc=1, device_id=where, device_id_type=pl.DeviceIdType.MESH)

    for step in range(1, heads):
        greet((section, replica, head_at(step)))
    for step in range(1, replicas):
        greet((section, replica_at(step), me))

    @pl.when(not_first)
    def _():
        greet((section - 1, replica, me))

    @pl.when(not_last)
    def _():
        greet((section + 1, replica, me))

    pl.semaphore_wait(
        barrier,
        heads - 1 + replicas - 1 + not_first.astype(jnp.int32) + not_last.astype(jnp.int32),
    )

    x_copies = []
    for step in range(1, heads):
        copy = remote(
            x_hbm.at[0],
            x1.at[me],
            x_send.at[step - 1],
            x_recv.at[step - 1],
            (section, replica, head_at(step)),
        )
        copy.start()
        x_copies.append(copy)
    value_copy = remote(f1, f2, v_send.at[0], v_recv.at[0], (section + 1, replica, me))

    gain_load.wait()
    x_load.wait()
    for copy in x_copies:
        copy.wait_recv()
    squares = jnp.zeros((tokens, 1), F32)
    for h in range(heads):
        part = x1[h].astype(F32)
        squares += jnp.sum(part * part, axis=-1, keepdims=True)
    inverse = lax.rsqrt(squares / model + EPSILON)
    for h in range(heads):
        columns = pl.ds(h * width, width)
        normed1[:, columns] = (x1[h].astype(F32) * inverse * gain[:, columns]).astype(BF16)

    def send_normed(normed, turn):
        copies = []
        for step in range(1, replicas):
            peer = replica_at(step)
            first = pl.multiple_of(peer * grad_rows, 128)
            copy = remote(
                normed.at[:, pl.ds(first, grad_rows)],
                rows_n.at[turn, replica],
                n_send.at[turn, step - 1],
                n_recv.at[turn, step - 1],
                (section, peer, me),
            )
            copy.start()
            copies.append(copy)
        first = pl.multiple_of(replica * grad_rows, 128)
        rows_n[turn, replica] = normed[:, pl.ds(first, grad_rows)]
        return copies

    n1_copies = send_normed(normed1, 0)
    c_copies = []
    for step in range(1, replicas):
        copy = remote(
            cot_hbm.at[0],
            rows_c.at[replica],
            c_send.at[step - 1],
            c_recv.at[step - 1],
            (section, replica_at(step), me),
        )
        copy.start()
        c_copies.append(copy)

    k_at, v_at = q_width, q_width + kv_width
    wk_load.wait()
    acc[:, pl.ds(k_at, kv_width)] = dot(normed1[...], wk[...])
    wv_load.wait()
    acc[:, pl.ds(v_at, kv_width)] = dot(normed1[...], wv[...])
    for load in wq_loads:
        load.wait()

    def query_tile(i, _):
        columns = pl.ds(pl.multiple_of(i * CHUNK, CHUNK), CHUNK)
        acc[:, columns] = dot(normed1[...], wq[:, columns])
        return 0

    lax.fori_loop(0, q_width // CHUNK, query_tile, 0)

    seg_load.wait()
    scale_load.wait()
    blend_load.wait()

    @pl.when(not_first)
    def _():
        f1_load.wait()

    @pl.when(is_first)
    def _():
        f1[...] = acc[:, pl.ds(v_at, kv_width)].astype(BF16)

    @pl.when(not_last)
    def _():
        value_copy.start()

    causal = lax.broadcasted_iota(jnp.int32, (tokens, tokens), 0) >= lax.broadcasted_iota(
        jnp.int32, (tokens, tokens), 1
    )

    def attend(segment_index, earlier, att, turn):
        row = seg[pl.ds(segment_index, 1), :].astype(F32)
        across = jnp.broadcast_to(row, (tokens, tokens))
        allowed = causal & (across == across.T)
        for g in range(kv_heads):
            kv_columns = pl.ds(g * HEAD_WIDTH, HEAD_WIDTH)
            values = acc[:, pl.ds(v_at + g * HEAD_WIDTH, HEAD_WIDTH)]
            blended = values + blend[:, g : g + 1] * earlier[:, kv_columns].astype(F32)
            mixed_values = jnp.where(is_first, values, blended).astype(BF16)
            key_high, key_low = split_high_low(
                rms_rows(acc[:, pl.ds(k_at + g * HEAD_WIDTH, HEAD_WIDTH)])
            )
            keys = jnp.concatenate([key_high, key_high, key_low], axis=1)
            queries = []
            for j in range(group):
                h = g * group + j
                query_high, query_low = split_high_low(
                    rms_rows(acc[:, pl.ds(h * HEAD_WIDTH, HEAD_WIDTH)])
                    * (scale[:, h : h + 1] / math.sqrt(HEAD_WIDTH))
                )
                queries.append(jnp.concatenate([query_high, query_low, query_high], axis=1))
            scores = lax.dot_general(
                jnp.concatenate(queries, axis=0),
                keys,
                (((1,), (1,)), ((), ())),
                preferred_element_type=F32,
            ).reshape(group, tokens, tokens)
            scores = jnp.where(allowed[None], scores, -1e30)
            exponent = jnp.exp(scores - jnp.max(scores, axis=-1, keepdims=True))
            weights = (exponent / jnp.sum(exponent, axis=-1, keepdims=True)).astype(BF16)
            result = dot(weights.reshape(group * tokens, tokens), mixed_values).astype(BF16)
            for j in range(group):
                att[me, :, pl.ds((g * group + j) * HEAD_WIDTH, HEAD_WIDTH)] = result[
                    j * tokens : (j + 1) * tokens
                ]
            columns = pl.ds(g * group * HEAD_WIDTH, group * HEAD_WIDTH)
            for step in range(1, heads):
                copy = remote(
                    att.at[me, :, columns],
                    att.at[me, :, columns],
                    a_send.at[turn, step - 1, g],
                    a_recv.at[turn, step - 1, g],
                    (section, replica, head_at(step)),
                )
                copy.start()
                a_copies.append((turn, copy))

    a_copies = []
    attend(section, f1, att1, 0)

    def own_part(att):
        rows = pl.ds(pl.multiple_of(me * q_width, q_width), q_width)

        def tile(i, _):
            columns = pl.ds(pl.multiple_of(i * CHUNK, CHUNK), CHUNK)
            proj[:, columns] = dot(att[me], wo[rows, columns])
            return 0

        lax.fori_loop(0, chunks, tile, 0)

    def whole_tile(att, stream, columns):
        total = proj[:, columns] + stream[me, :, columns].astype(F32)
        for step in range(1, heads):
            peer = lax.rem(me + heads - step, heads)
            rows = pl.ds(pl.multiple_of(peer * q_width, q_width), q_width)
            total += dot(att[peer], wo[rows, columns])
        return total.astype(BF16)

    def z_copy(c):
        columns = pl.ds(c * CHUNK, CHUNK)
        return remote(
            out1.at[:, columns],
            x2.at[me, :, columns],
            z_send.at[c],
            z_recv.at[c],
            (section + 1, replica, me),
        )

    for load in wo_loads:
        load.wait()
    own_part(att1)
    for turn, copy in a_copies:
        if turn == 0:
            copy.wait_recv()
    for c in range(chunks):
        columns = pl.ds(c * CHUNK, CHUNK)
        out1[:, columns] = whole_tile(att1, x1, columns)

        @pl.when(not_last)
        def _(c=c):
            z_copy(c).start()

    out1_store = local(out1, out1_hbm.at[0], out_sem.at[0])

    cot_load.wait()
    for copy in c_copies + n1_copies:
        copy.wait_recv()

    def grad_part(turn):
        total = jnp.zeros(grad.shape, F32)
        for p in range(replicas):
            total += lax.dot_general(
                rows_n[turn, p],
                rows_c[p, turn],
                (((0,), (0,)), ((), ())),
                preferred_element_type=F32,
            )
        return total

    grad[...] = grad_part(0)

    def forward(step, c):
        columns = pl.ds(c * CHUNK, CHUNK)
        return remote(
            x2.at[me, :, columns],
            x2.at[me, :, columns],
            f_send.at[step - 1, c],
            f_recv.at[step - 1, c],
            (section, replica, head_at(step)),
        )

    @pl.when(is_first)
    def _():
        for load in enter_loads:
            load.wait()

    squares = jnp.zeros((tokens, 1), F32)
    for c in range(chunks):
        columns = pl.ds(c * CHUNK, CHUNK)

        @pl.when(not_first)
        def _(c=c):
            z_copy(c).wait_recv()
            for step in range(1, heads):
                forward(step, c).start()

        for step in range(heads):
            owner = lax.rem(me + heads - step, heads)
            if step > 0:

                @pl.when(not_first)
                def _(step=step, c=c):
                    forward(step, c).wait_recv()

            rows = pl.ds(pl.multiple_of(owner * width + c * CHUNK, CHUNK), CHUNK)
            part = x2[owner, :, columns].astype(F32)
            squares += jnp.sum(part * part, axis=-1, keepdims=True)
            scaled = (part * gain[:, rows]).astype(BF16)
            for weight, at, size in (
                (wk, k_at, kv_width),
                (wv, v_at, kv_width),
                (wq, 0, q_width),
            ):
                product = dot(scaled, weight[rows, :])
                if c == 0 and step == 0:
                    acc[:, pl.ds(at, size)] = product
                else:
                    acc[:, pl.ds(at, size)] += product
    inverse = lax.rsqrt(squares / model + EPSILON)
    for h in range(heads):
        columns = pl.ds(h * width, width)
        normed2[:, columns] = (x2[h].astype(F32) * inverse * gain[:, columns]).astype(BF16)
    n2_copies = send_normed(normed2, 1)
    acc[...] = acc[...] * inverse

    @pl.when(not_first)
    def _():
        value_copy.wait_recv()

    attend(lax.rem(section + sections, sections + 1), f2, att2, 1)
    own_part(att2)
    for turn, copy in a_copies:
        if turn == 1:
            copy.wait_recv()
    for c in range(chunks):
        columns = pl.ds(c * CHUNK, CHUNK)
        out2[:, columns] = whole_tile(att2, x2, columns)
    out2_store = local(out2, out2_hbm.at[0], out_sem.at[1])

    for copy in n2_copies:
        copy.wait_recv()
    grad[...] += grad_part(1)
    grad_store = local(grad, grad_hbm.at[0], out_sem.at[2])

    for copy in x_copies + c_copies + n1_copies + n2_copies:
        copy.wait_send()
    for _, copy in a_copies:
        copy.wait_send()

    @pl.when(not_last)
    def _():
        value_copy.wait_send()
        for c in range(chunks):
            z_copy(c).wait_send()

    @pl.when(not_first)
    def _():
        for c in range(chunks):
            for step in range(1, heads):
                forward(step, c).wait_send()

    out1_store.wait()
    out2_store.wait()
    grad_store.wait()


def solution(mesh):
    sections, replicas, heads = (mesh.shape[a] for a in ("section", "dp", "head"))

    def per_device(
        segments,
        stream,
        entering,
        pending,
        gain,
        wq,
        wk,
        wv,
        wo,
        scale,
        blend,
        cotangent,
    ):
        _, tokens, width = stream.shape
        model = width * heads
        q_width, kv_width = wq.shape[2], wk.shape[2]
        grad_rows = model // replicas
        chunks = width // CHUNK
        kv_heads = kv_width // HEAD_WIDTH
        others = heads - 1
        peers = replicas - 1
        dma = pltpu.SemaphoreType.DMA
        scratch = [
            pltpu.VMEM(segments.shape, jnp.int32),
            pltpu.VMEM(gain.shape, F32),
            pltpu.VMEM(scale.shape, F32),
            pltpu.VMEM(blend.shape, F32),
            pltpu.VMEM((model, q_width), BF16),
            pltpu.VMEM((model, kv_width), BF16),
            pltpu.VMEM((model, kv_width), BF16),
            pltpu.VMEM((model, width), BF16),
            pltpu.VMEM((heads, tokens, width), BF16),
            pltpu.VMEM((heads, tokens, width), BF16),
            pltpu.VMEM((tokens, kv_width), BF16),
            pltpu.VMEM((tokens, kv_width), BF16),
            pltpu.VMEM((tokens, model), BF16),
            pltpu.VMEM((tokens, model), BF16),
            pltpu.VMEM((tokens, q_width + 2 * kv_width), F32),
            pltpu.VMEM((heads, tokens, q_width), BF16),
            pltpu.VMEM((heads, tokens, q_width), BF16),
            pltpu.VMEM((tokens, width), BF16),
            pltpu.VMEM((tokens, width), BF16),
            pltpu.VMEM((tokens, width), F32),
            pltpu.VMEM((2, replicas, tokens, grad_rows), BF16),
            pltpu.VMEM((replicas, 2, tokens, kv_width), BF16),
            pltpu.VMEM((grad_rows, kv_width), F32),
            dma((7,)),
            dma((10,)),
            dma((heads,)),
            dma((3,)),
            dma((others,)),
            dma((others,)),
            dma((peers,)),
            dma((peers,)),
            dma((2, peers)),
            dma((2, peers)),
            dma((2, others, kv_heads)),
            dma((2, others, kv_heads)),
            dma((chunks,)),
            dma((chunks,)),
            dma((others, chunks)),
            dma((others, chunks)),
            dma((1,)),
            dma((1,)),
        ]
        return pl.pallas_call(
            functools.partial(kernel, sections, replicas, heads),
            out_shape=(
                jax.ShapeDtypeStruct(stream.shape, BF16),
                jax.ShapeDtypeStruct(stream.shape, BF16),
                jax.ShapeDtypeStruct((1, grad_rows, kv_width), F32),
            ),
            in_specs=[pl.BlockSpec(memory_space=pl.ANY)] * 12,
            out_specs=(pl.BlockSpec(memory_space=pl.ANY),) * 3,
            scratch_shapes=scratch,
            compiler_params=pltpu.CompilerParams(
                collective_id=0, has_side_effects=True, vmem_limit_bytes=56 * 1024 * 1024
            ),
        )(
            segments,
            stream,
            entering,
            pending,
            gain,
            wq,
            wk,
            wv,
            wo,
            scale,
            blend,
            cotangent,
        )

    return jax.shard_map(
        per_device,
        mesh=mesh,
        in_specs=(
            P(None, "dp"),
            P("section", "dp", "head"),
            P("dp", None),
            P("section", "dp", "head"),
            P("section", None),
            P("section", None, "head"),
            P("section", None, "head"),
            P("section", None, "head"),
            P("section", None, "head"),
            P("section", "head"),
            P("section", "head"),
            P("section", None, "dp", "head"),
        ),
        out_specs=(
            P("section", "dp", "head"),
            P("section", "dp", "head"),
            P("section", "dp", "head"),
        ),
        check_vma=False,
    )
```

```python
import functools
import math

import jax
import jax.numpy as jnp
from jax import lax
from jax.experimental import pallas as pl
from jax.experimental.pallas import tpu as pltpu
from jax.sharding import PartitionSpec as P

HEAD_WIDTH = 128
CHUNK = 256
EPSILON = 1e-06
F32 = jnp.float32
BF16 = jnp.bfloat16


def dot(a, b):
    return jnp.dot(a, b, preferred_element_type=F32)


def split_high_low(values):
    high = values.astype(BF16)
    return high, (values - high.astype(F32)).astype(BF16)


def kernel(
    sections,
    replicas,
    heads,
    seg_hbm,
    x_hbm,
    entering_hbm,
    pending_hbm,
    gain_hbm,
    wq_hbm,
    wk_hbm,
    wv_hbm,
    wo_hbm,
    scale_hbm,
    blend_hbm,
    cot_hbm,
    out1_hbm,
    out2_hbm,
    grad_hbm,
    seg,
    gain,
    scale,
    blend,
    wq,
    wk,
    wv,
    wo,
    x1,
    x2,
    f1,
    f2,
    normed1,
    normed2,
    acc,
    att1,
    att2,
    out1,
    out2,
    proj,
    rows_n,
    rows_c,
    grad,
    local_sem,
    weight_sem,
    enter_sem,
    out_sem,
    x_send,
    x_recv,
    c_send,
    c_recv,
    n_send,
    n_recv,
    a_send,
    a_recv,
    z_send,
    z_recv,
    f_send,
    f_recv,
    v_send,
    v_recv,
):
    section = lax.axis_index("section")
    replica = lax.axis_index("dp")
    me = lax.axis_index("head")
    tokens, width = x1.shape[1], x1.shape[2]
    model = width * heads
    q_width, kv_width = wq.shape[1], wk.shape[1]
    kv_heads = kv_width // HEAD_WIDTH
    group = q_width // kv_width
    grad_rows = model // replicas
    chunks = width // CHUNK
    is_first = section == 0
    not_first = section > 0
    not_last = section < sections - 1

    def local(src, dst, sem):
        copy = pltpu.make_async_copy(src, dst, sem)
        copy.start()
        return copy

    def remote(src, dst, send, recv, where):
        return pltpu.make_async_remote_copy(
            src_ref=src,
            dst_ref=dst,
            send_sem=send,
            recv_sem=recv,
            device_id=where,
            device_id_type=pl.DeviceIdType.MESH,
        )

    def head_at(step):
        return lax.rem(me + step, heads)

    def replica_at(step):
        return lax.rem(replica + step, replicas)

    x_load = local(x_hbm.at[0], x1.at[me], local_sem.at[0])
    gain_load = local(gain_hbm, gain, local_sem.at[1])
    wk_load = local(wk_hbm.at[0], wk, weight_sem.at[0])
    wv_load = local(wv_hbm.at[0], wv, weight_sem.at[1])
    quarter = model // 4
    wq_loads = [
        local(
            wq_hbm.at[0, pl.ds(i * quarter, quarter)],
            wq.at[pl.ds(i * quarter, quarter)],
            weight_sem.at[2 + i],
        )
        for i in range(4)
    ]
    seg_load = local(seg_hbm, seg, local_sem.at[2])
    scale_load = local(scale_hbm, scale, local_sem.at[3])
    blend_load = local(blend_hbm, blend, local_sem.at[4])
    cot_load = local(cot_hbm.at[0], rows_c.at[replica], local_sem.at[5])
    f1_load = pltpu.make_async_copy(pending_hbm.at[0], f1, local_sem.at[6])

    @pl.when(not_first)
    def _():
        f1_load.start()

    wo_loads = [
        local(
            wo_hbm.at[0, pl.ds(i * quarter, quarter)],
            wo.at[pl.ds(i * quarter, quarter)],
            weight_sem.at[6 + i],
        )
        for i in range(4)
    ]
    enter_loads = [
        pltpu.make_async_copy(
            entering_hbm.at[:, pl.ds(h * width, width)], x2.at[h], enter_sem.at[h]
        )
        for h in range(heads)
    ]

    @pl.when(is_first)
    def _():
        for load in enter_loads:
            load.start()
        f2[...] = jnp.zeros_like(f2)

    barrier = pltpu.get_barrier_semaphore()

    def greet(where):
        pl.semaphore_signal(barrier, inc=1, device_id=where, device_id_type=pl.DeviceIdType.MESH)

    for step in range(1, heads):
        greet((section, replica, head_at(step)))
    for step in range(1, replicas):
        greet((section, replica_at(step), me))

    @pl.when(not_first)
    def _():
        greet((section - 1, replica, me))

    @pl.when(not_last)
    def _():
        greet((section + 1, replica, me))

    pl.semaphore_wait(
        barrier,
        heads - 1 + replicas - 1 + not_first.astype(jnp.int32) + not_last.astype(jnp.int32),
    )

    x_copies = []
    for step in range(1, heads):
        copy = remote(
            x_hbm.at[0],
            x1.at[me],
            x_send.at[step - 1],
            x_recv.at[step - 1],
            (section, replica, head_at(step)),
        )
        copy.start()
        x_copies.append(copy)
    value_copy = remote(f1, f2, v_send.at[0], v_recv.at[0], (section + 1, replica, me))

    c_copies = []
    for step in range(1, replicas):
        copy = remote(
            cot_hbm.at[0],
            rows_c.at[replica],
            c_send.at[step - 1],
            c_recv.at[step - 1],
            (section, replica_at(step), me),
        )
        copy.start()
        c_copies.append(copy)

    k_at, v_at = q_width, q_width + kv_width
    weights_at = ((wk, k_at, kv_width), (wv, v_at, kv_width), (wq, 0, q_width))

    def project(part, first_row, size, is_start):
        rows = pl.ds(pl.multiple_of(first_row, CHUNK), size)
        scaled = (part * gain[:, rows]).astype(BF16)
        for weight, at, columns in weights_at:
            product = dot(scaled, weight[rows, :])
            if is_start:
                acc[:, pl.ds(at, columns)] = product
            else:
                acc[:, pl.ds(at, columns)] += product

    def normalize(stream, squares, normed):
        inverse = lax.rsqrt(squares / model + EPSILON)
        for h in range(heads):
            columns = pl.ds(h * width, width)
            normed[:, columns] = (stream[h].astype(F32) * inverse * gain[:, columns]).astype(BF16)
        return inverse

    def send_normed(normed, turn):
        copies = []
        for step in range(1, replicas):
            peer = replica_at(step)
            first = pl.multiple_of(peer * grad_rows, 128)
            copy = remote(
                normed.at[:, pl.ds(first, grad_rows)],
                rows_n.at[turn, replica],
                n_send.at[turn, step - 1],
                n_recv.at[turn, step - 1],
                (section, peer, me),
            )
            copy.start()
            copies.append(copy)
        first = pl.multiple_of(replica * grad_rows, 128)
        rows_n[turn, replica] = normed[:, pl.ds(first, grad_rows)]
        return copies

    gain_load.wait()
    x_load.wait()
    wk_load.wait()
    wv_load.wait()
    for load in wq_loads:
        load.wait()
    part = x1[me].astype(F32)
    squares = jnp.sum(part * part, axis=-1, keepdims=True)
    project(part, me * width, width, True)
    for copy in x_copies:
        copy.wait_recv()
    for step in range(1, heads):
        part = x1[lax.rem(me + heads - step, heads)].astype(F32)
        squares += jnp.sum(part * part, axis=-1, keepdims=True)
    inverse1 = normalize(x1, squares, normed1)
    n1_copies = send_normed(normed1, 0)
    for step in range(1, heads):
        owner = lax.rem(me + heads - step, heads)
        project(x1[owner].astype(F32), owner * width, width, False)

    seg_load.wait()
    scale_load.wait()
    blend_load.wait()

    @pl.when(not_first)
    def _():
        f1_load.wait()

    @pl.when(is_first)
    def _():
        f1[...] = (acc[:, pl.ds(v_at, kv_width)] * inverse1).astype(BF16)

    @pl.when(not_last)
    def _():
        value_copy.start()

    causal = lax.broadcasted_iota(jnp.int32, (tokens, tokens), 0) >= lax.broadcasted_iota(
        jnp.int32, (tokens, tokens), 1
    )

    ones = jnp.ones((2 * HEAD_WIDTH, HEAD_WIDTH), BF16)
    mixed_ones = jnp.ones((tokens, HEAD_WIDTH), BF16)

    def unit_rows(values):
        total = dot(jnp.concatenate(split_high_low(values * values), axis=1), ones)
        return values * lax.rsqrt(total / HEAD_WIDTH + EPSILON)

    def attend(segment_index, earlier, att, turn, inverse):
        row = seg[pl.ds(segment_index, 1), :].astype(F32)
        across = jnp.broadcast_to(row, (tokens, tokens))
        allowed = causal & (across == across.T)
        for g in range(kv_heads):
            kv_columns = pl.ds(g * HEAD_WIDTH, HEAD_WIDTH)
            values = acc[:, pl.ds(v_at + g * HEAD_WIDTH, HEAD_WIDTH)] * inverse
            blended = values + blend[:, g : g + 1] * earlier[:, kv_columns].astype(F32)
            mixed_values = jnp.where(is_first, values, blended).astype(BF16)
            key_high, key_low = split_high_low(
                unit_rows(acc[:, pl.ds(k_at + g * HEAD_WIDTH, HEAD_WIDTH)] * inverse)
            )
            keys = jnp.concatenate([key_high, key_high, key_low], axis=1)
            queries = []
            for j in range(group):
                h = g * group + j
                query_high, query_low = split_high_low(
                    unit_rows(acc[:, pl.ds(h * HEAD_WIDTH, HEAD_WIDTH)] * inverse)
                    * (scale[:, h : h + 1] / math.sqrt(HEAD_WIDTH))
                )
                queries.append(jnp.concatenate([query_high, query_low, query_high], axis=1))
            scores = lax.dot_general(
                jnp.concatenate(queries, axis=0),
                keys,
                (((1,), (1,)), ((), ())),
                preferred_element_type=F32,
            ).reshape(group, tokens, tokens)
            scores = jnp.where(allowed[None], scores, -1e30)
            exponent = jnp.exp(scores - jnp.max(scores, axis=-1, keepdims=True)).astype(BF16)
            result = dot(
                exponent.reshape(group * tokens, tokens),
                jnp.concatenate([mixed_values, mixed_ones], axis=1),
            )
            result = (result[:, :HEAD_WIDTH] / result[:, HEAD_WIDTH:]).astype(BF16)
            for j in range(group):
                att[me, :, pl.ds((g * group + j) * HEAD_WIDTH, HEAD_WIDTH)] = result[
                    j * tokens : (j + 1) * tokens
                ]
            columns = pl.ds(g * group * HEAD_WIDTH, group * HEAD_WIDTH)
            for step in range(1, heads):
                copy = remote(
                    att.at[me, :, columns],
                    att.at[me, :, columns],
                    a_send.at[turn, step - 1, g],
                    a_recv.at[turn, step - 1, g],
                    (section, replica, head_at(step)),
                )
                copy.start()
                a_copies.append((turn, copy))

    a_copies = []
    attend(section, f1, att1, 0, inverse1)

    def own_tile(att, c):
        rows = pl.ds(pl.multiple_of(me * q_width, q_width), q_width)
        columns = pl.ds(c * CHUNK, CHUNK)
        proj[:, columns] = dot(att[me], wo[rows, columns])

    def whole_tile(att, stream, c):
        columns = pl.ds(c * CHUNK, CHUNK)
        total = proj[:, columns] + stream[me, :, columns].astype(F32)
        for step in range(1, heads):
            peer = lax.rem(me + heads - step, heads)
            rows = pl.ds(pl.multiple_of(peer * q_width, q_width), q_width)
            total += dot(att[peer], wo[rows, columns])
        return total.astype(BF16)

    def z_copy(c):
        columns = pl.ds(c * CHUNK, CHUNK)
        return remote(
            out1.at[:, columns],
            x2.at[me, :, columns],
            z_send.at[c],
            z_recv.at[c],
            (section + 1, replica, me),
        )

    for load in wo_loads:
        load.wait()
    ahead = chunks // 2
    for c in range(ahead):
        own_tile(att1, c)
    for turn, copy in a_copies:
        if turn == 0:
            copy.wait_recv()
    for c in range(chunks):
        if c >= ahead:
            own_tile(att1, c)
        out1[:, pl.ds(c * CHUNK, CHUNK)] = whole_tile(att1, x1, c)

        @pl.when(not_last)
        def _(c=c):
            z_copy(c).start()

    out1_store = local(out1, out1_hbm.at[0], out_sem.at[0])

    def grad_part(turn, step):
        p = lax.rem(replica + replicas - step, replicas)
        return lax.dot_general(
            rows_n[turn, p],
            rows_c[p, turn],
            (((0,), (0,)), ((), ())),
            preferred_element_type=F32,
        )

    cot_load.wait()
    grad[...] = grad_part(0, 0)

    def forward(step, c):
        columns = pl.ds(c * CHUNK, CHUNK)
        return remote(
            x2.at[me, :, columns],
            x2.at[me, :, columns],
            f_send.at[step - 1, c],
            f_recv.at[step - 1, c],
            (section, replica, head_at(step)),
        )

    @pl.when(is_first)
    def _():
        for load in enter_loads:
            load.wait()

    squares = jnp.zeros((tokens, 1), F32)
    for c in range(chunks):
        columns = pl.ds(c * CHUNK, CHUNK)

        @pl.when(not_first)
        def _(c=c):
            z_copy(c).wait_recv()
            for step in range(1, heads):
                forward(step, c).start()

        part = x2[me, :, columns].astype(F32)
        squares += jnp.sum(part * part, axis=-1, keepdims=True)
        project(part, me * width + c * CHUNK, CHUNK, c == 0)
        if c < chunks - 1:
            for step in range(1 + c * (replicas - 1) // (chunks - 1), 1 + (c + 1) * (replicas - 1) // (chunks - 1)):
                c_copies[step - 1].wait_recv()
                n1_copies[step - 1].wait_recv()
                grad[...] += grad_part(0, step)

        @pl.when(not_first)
        def _(c=c):
            for step in range(1, heads):
                forward(step, c).wait_recv()

        parts = [x2[lax.rem(me + heads - step, heads), :, columns].astype(F32) for step in range(1, heads)]
        for part in parts:
            squares += jnp.sum(part * part, axis=-1, keepdims=True)
        if c == chunks - 1:
            inverse2 = normalize(x2, squares, normed2)
            n2_copies = send_normed(normed2, 1)
        for step in range(1, heads):
            owner = lax.rem(me + heads - step, heads)
            project(parts[step - 1], owner * width + c * CHUNK, CHUNK, False)

    @pl.when(not_first)
    def _():
        value_copy.wait_recv()

    attend(lax.rem(section + sections, sections + 1), f2, att2, 1, inverse2)
    for c in range(chunks):
        own_tile(att2, c)
    for turn, copy in a_copies:
        if turn == 1:
            copy.wait_recv()
    for c in range(chunks):
        out2[:, pl.ds(c * CHUNK, CHUNK)] = whole_tile(att2, x2, c)
    out2_store = local(out2, out2_hbm.at[0], out_sem.at[1])

    total = grad[...] + grad_part(1, 0)
    for step in range(1, replicas):
        n2_copies[step - 1].wait_recv()
        total += grad_part(1, step)
    grad[...] = total
    grad_store = local(grad, grad_hbm.at[0], out_sem.at[2])

    for copy in x_copies + c_copies + n1_copies + n2_copies:
        copy.wait_send()
    for _, copy in a_copies:
        copy.wait_send()

    @pl.when(not_last)
    def _():
        value_copy.wait_send()
        for c in range(chunks):
            z_copy(c).wait_send()

    @pl.when(not_first)
    def _():
        for c in range(chunks):
            for step in range(1, heads):
                forward(step, c).wait_send()

    out1_store.wait()
    out2_store.wait()
    grad_store.wait()


def store_kernel(*refs):
    sources, targets, sems = refs[:3], refs[3:6], refs[6]
    copies = []
    for source, target in zip(sources, targets):
        rows = source.shape[1] // 2
        for i in range(2):
            block = pl.ds(i * rows, rows)
            copy = pltpu.make_async_copy(
                source.at[0, block], target.at[0, block], sems.at[len(copies)]
            )
            copy.start()
            copies.append(copy)
    for copy in copies:
        copy.wait()


def solution(mesh):
    sections, replicas, heads = (mesh.shape[a] for a in ("section", "dp", "head"))

    def per_device(
        segments,
        stream,
        entering,
        pending,
        gain,
        wq,
        wk,
        wv,
        wo,
        scale,
        blend,
        cotangent,
    ):
        _, tokens, width = stream.shape
        model = width * heads
        q_width, kv_width = wq.shape[2], wk.shape[2]
        grad_rows = model // replicas
        chunks = width // CHUNK
        kv_heads = kv_width // HEAD_WIDTH
        others = heads - 1
        peers = replicas - 1
        dma = pltpu.SemaphoreType.DMA
        scratch = [
            pltpu.VMEM(segments.shape, jnp.int32),
            pltpu.VMEM(gain.shape, F32),
            pltpu.VMEM(scale.shape, F32),
            pltpu.VMEM(blend.shape, F32),
            pltpu.VMEM((model, q_width), BF16),
            pltpu.VMEM((model, kv_width), BF16),
            pltpu.VMEM((model, kv_width), BF16),
            pltpu.VMEM((model, width), BF16),
            pltpu.VMEM((heads, tokens, width), BF16),
            pltpu.VMEM((heads, tokens, width), BF16),
            pltpu.VMEM((tokens, kv_width), BF16),
            pltpu.VMEM((tokens, kv_width), BF16),
            pltpu.VMEM((tokens, model), BF16),
            pltpu.VMEM((tokens, model), BF16),
            pltpu.VMEM((tokens, q_width + 2 * kv_width), F32),
            pltpu.VMEM((heads, tokens, q_width), BF16),
            pltpu.VMEM((heads, tokens, q_width), BF16),
            pltpu.VMEM((tokens, width), BF16),
            pltpu.VMEM((tokens, width), BF16),
            pltpu.VMEM((tokens, width), F32),
            pltpu.VMEM((2, replicas, tokens, grad_rows), BF16),
            pltpu.VMEM((replicas, 2, tokens, kv_width), BF16),
            pltpu.VMEM((grad_rows, kv_width), F32),
            dma((7,)),
            dma((10,)),
            dma((heads,)),
            dma((3,)),
            dma((others,)),
            dma((others,)),
            dma((peers,)),
            dma((peers,)),
            dma((2, peers)),
            dma((2, peers)),
            dma((2, others, kv_heads)),
            dma((2, others, kv_heads)),
            dma((chunks,)),
            dma((chunks,)),
            dma((others, chunks)),
            dma((others, chunks)),
            dma((1,)),
            dma((1,)),
        ]
        results = pl.pallas_call(
            functools.partial(kernel, sections, replicas, heads),
            out_shape=(
                jax.ShapeDtypeStruct(stream.shape, BF16),
                jax.ShapeDtypeStruct(stream.shape, BF16),
                jax.ShapeDtypeStruct((1, grad_rows, kv_width), F32),
            ),
            in_specs=[pl.BlockSpec(memory_space=pl.ANY)] * 12,
            out_specs=(pl.BlockSpec(memory_space=pl.ANY),) * 3,
            scratch_shapes=scratch,
            compiler_params=pltpu.CompilerParams(
                collective_id=0, has_side_effects=True, vmem_limit_bytes=56 * 1024 * 1024
            ),
        )(
            segments,
            stream,
            entering,
            pending,
            gain,
            wq,
            wk,
            wv,
            wo,
            scale,
            blend,
            cotangent,
        )
        return pl.pallas_call(
            store_kernel,
            out_shape=tuple(jax.ShapeDtypeStruct(r.shape, r.dtype) for r in results),
            in_specs=[pl.BlockSpec(memory_space=pl.ANY)] * 3,
            out_specs=(pl.BlockSpec(memory_space=pl.ANY),) * 3,
            scratch_shapes=[dma((6,))],
            compiler_params=pltpu.CompilerParams(vmem_limit_bytes=56 * 1024 * 1024),
        )(*results)

    return jax.shard_map(
        per_device,
        mesh=mesh,
        in_specs=(
            P(None, "dp"),
            P("section", "dp", "head"),
            P("dp", None),
            P("section", "dp", "head"),
            P("section", None),
            P("section", None, "head"),
            P("section", None, "head"),
            P("section", None, "head"),
            P("section", None, "head"),
            P("section", "head"),
            P("section", "head"),
            P("section", None, "dp", "head"),
        ),
        out_specs=(
            P("section", "dp", "head"),
            P("section", "dp", "head"),
            P("section", "dp", "head"),
        ),
        check_vma=False,
    )
```

```python
import functools
import math

import jax
import jax.numpy as jnp
from jax import lax
from jax.experimental import pallas as pl
from jax.experimental.pallas import tpu as pltpu
from jax.sharding import PartitionSpec as P

HEAD_WIDTH = 128
CHUNK = 256
STORE_BLOCKS = 2
EPSILON = 1e-06
F32 = jnp.float32
BF16 = jnp.bfloat16


def dot(a, b):
    return jnp.dot(a, b, preferred_element_type=F32)


def split_high_low(values):
    high = values.astype(BF16)
    return high, (values - high.astype(F32)).astype(BF16)


def kernel(
    sections,
    replicas,
    heads,
    seg_hbm,
    x_hbm,
    entering_hbm,
    pending_hbm,
    gain_hbm,
    wq_hbm,
    wk_hbm,
    wv_hbm,
    wo_hbm,
    scale_hbm,
    blend_hbm,
    cot_hbm,
    out1_hbm,
    out2_hbm,
    grad_hbm,
    seg,
    gain,
    scale,
    blend,
    wq,
    wk,
    wv,
    wo,
    x1,
    x2,
    f1,
    f2,
    normed1,
    normed2,
    acc,
    att1,
    att2,
    out1,
    out2,
    proj,
    rows_n,
    rows_c,
    grad,
    local_sem,
    weight_sem,
    enter_sem,
    out_sem,
    x_send,
    x_recv,
    c_send,
    c_recv,
    n_send,
    n_recv,
    a_send,
    a_recv,
    z_send,
    z_recv,
    f_send,
    f_recv,
    v_send,
    v_recv,
):
    section = lax.axis_index("section")
    replica = lax.axis_index("dp")
    me = lax.axis_index("head")
    tokens, width = x1.shape[1], x1.shape[2]
    model = width * heads
    q_width, kv_width = wq.shape[1], wk.shape[1]
    kv_heads = kv_width // HEAD_WIDTH
    group = q_width // kv_width
    grad_rows = model // replicas
    chunks = width // CHUNK
    is_first = section == 0
    not_first = section > 0
    not_last = section < sections - 1

    def local(src, dst, sem):
        copy = pltpu.make_async_copy(src, dst, sem)
        copy.start()
        return copy

    def remote(src, dst, send, recv, where):
        return pltpu.make_async_remote_copy(
            src_ref=src,
            dst_ref=dst,
            send_sem=send,
            recv_sem=recv,
            device_id=where,
            device_id_type=pl.DeviceIdType.MESH,
        )

    def head_at(step):
        return lax.rem(me + step, heads)

    def replica_at(step):
        return lax.rem(replica + step, replicas)

    x_load = local(x_hbm.at[0], x1.at[me], local_sem.at[0])
    gain_load = local(gain_hbm, gain, local_sem.at[1])
    weight_loads = []
    for step in range(heads):
        first = pl.multiple_of(lax.rem(me + heads - step, heads) * width, CHUNK)
        half = width // 2
        blocks = [(wk_hbm, wk, first, width), (wv_hbm, wv, first, width)]
        blocks += [(wq_hbm, wq, first + i * half, half) for i in range(2)]
        weight_loads.append(
            [
                local(
                    source.at[0, pl.ds(pl.multiple_of(row, CHUNK), size)],
                    target.at[pl.ds(pl.multiple_of(row, CHUNK), size)],
                    weight_sem.at[4 * step + i],
                )
                for i, (source, target, row, size) in enumerate(blocks)
            ]
        )
    seg_load = local(seg_hbm, seg, local_sem.at[2])
    scale_load = local(scale_hbm, scale, local_sem.at[3])
    blend_load = local(blend_hbm, blend, local_sem.at[4])
    cot_load = local(cot_hbm.at[0], rows_c.at[replica], local_sem.at[5])
    f1_load = pltpu.make_async_copy(pending_hbm.at[0], f1, local_sem.at[6])

    @pl.when(not_first)
    def _():
        f1_load.start()

    quarter = model // 4
    wo_loads = [
        local(
            wo_hbm.at[0, pl.ds(i * quarter, quarter)],
            wo.at[pl.ds(i * quarter, quarter)],
            weight_sem.at[4 * heads + i],
        )
        for i in range(4)
    ]
    enter_loads = [
        pltpu.make_async_copy(
            entering_hbm.at[:, pl.ds(h * width, width)], x2.at[h], enter_sem.at[h]
        )
        for h in range(heads)
    ]

    @pl.when(is_first)
    def _():
        for load in enter_loads:
            load.start()
        f2[...] = jnp.zeros_like(f2)

    barrier = pltpu.get_barrier_semaphore()

    def greet(where):
        pl.semaphore_signal(barrier, inc=1, device_id=where, device_id_type=pl.DeviceIdType.MESH)

    for step in range(1, heads):
        greet((section, replica, head_at(step)))
    for step in range(1, replicas):
        greet((section, replica_at(step), me))

    @pl.when(not_first)
    def _():
        greet((section - 1, replica, me))

    @pl.when(not_last)
    def _():
        greet((section + 1, replica, me))

    pl.semaphore_wait(
        barrier,
        heads - 1 + replicas - 1 + not_first.astype(jnp.int32) + not_last.astype(jnp.int32),
    )

    x_copies = []
    for step in range(1, heads):
        copy = remote(
            x_hbm.at[0],
            x1.at[me],
            x_send.at[step - 1],
            x_recv.at[step - 1],
            (section, replica, head_at(step)),
        )
        copy.start()
        x_copies.append(copy)
    value_copy = remote(f1, f2, v_send.at[0], v_recv.at[0], (section + 1, replica, me))

    c_copies = []
    for step in range(1, replicas):
        copy = remote(
            cot_hbm.at[0],
            rows_c.at[replica],
            c_send.at[step - 1],
            c_recv.at[step - 1],
            (section, replica_at(step), me),
        )
        copy.start()
        c_copies.append(copy)

    k_at, v_at = q_width, q_width + kv_width
    weights_at = ((wk, k_at, kv_width), (wv, v_at, kv_width), (wq, 0, q_width))

    def project(part, first_row, size, is_start):
        rows = pl.ds(pl.multiple_of(first_row, CHUNK), size)
        scaled = (part * gain[:, rows]).astype(BF16)
        for weight, at, columns in weights_at:
            product = dot(scaled, weight[rows, :])
            if is_start:
                acc[:, pl.ds(at, columns)] = product
            else:
                acc[:, pl.ds(at, columns)] += product

    def normalize(stream, squares, normed):
        inverse = lax.rsqrt(squares / model + EPSILON)
        for h in range(heads):
            columns = pl.ds(h * width, width)
            normed[:, columns] = (stream[h].astype(F32) * inverse * gain[:, columns]).astype(BF16)
        return inverse

    def send_normed(normed, turn):
        copies = []
        for step in range(1, replicas):
            peer = replica_at(step)
            first = pl.multiple_of(peer * grad_rows, 128)
            copy = remote(
                normed.at[:, pl.ds(first, grad_rows)],
                rows_n.at[turn, replica],
                n_send.at[turn, step - 1],
                n_recv.at[turn, step - 1],
                (section, peer, me),
            )
            copy.start()
            copies.append(copy)
        first = pl.multiple_of(replica * grad_rows, 128)
        rows_n[turn, replica] = normed[:, pl.ds(first, grad_rows)]
        return copies

    gain_load.wait()
    x_load.wait()
    for load in weight_loads[0]:
        load.wait()
    part = x1[me].astype(F32)
    squares = jnp.sum(part * part, axis=-1, keepdims=True)
    project(part, me * width, width, True)
    for copy in x_copies:
        copy.wait_recv()
    for step in range(1, heads):
        part = x1[lax.rem(me + heads - step, heads)].astype(F32)
        squares += jnp.sum(part * part, axis=-1, keepdims=True)
    inverse1 = normalize(x1, squares, normed1)
    n1_copies = send_normed(normed1, 0)
    for step in range(1, heads):
        for load in weight_loads[step]:
            load.wait()
        owner = lax.rem(me + heads - step, heads)
        project(x1[owner].astype(F32), owner * width, width, False)

    seg_load.wait()
    scale_load.wait()
    blend_load.wait()

    @pl.when(not_first)
    def _():
        f1_load.wait()

    @pl.when(is_first)
    def _():
        f1[...] = (acc[:, pl.ds(v_at, kv_width)] * inverse1).astype(BF16)

    @pl.when(not_last)
    def _():
        value_copy.start()

    causal = lax.broadcasted_iota(jnp.int32, (tokens, tokens), 0) >= lax.broadcasted_iota(
        jnp.int32, (tokens, tokens), 1
    )

    ones = jnp.ones((2 * HEAD_WIDTH, HEAD_WIDTH), BF16)
    mixed_ones = jnp.ones((tokens, HEAD_WIDTH), BF16)

    def unit_rows(values):
        total = dot(jnp.concatenate(split_high_low(values * values), axis=1), ones)
        return values * lax.rsqrt(total / HEAD_WIDTH + EPSILON)

    def attend(segment_index, earlier, att, turn, inverse):
        row = seg[pl.ds(segment_index, 1), :].astype(F32)
        across = jnp.broadcast_to(row, (tokens, tokens))
        allowed = causal & (across == across.T)
        for g in range(kv_heads):
            kv_columns = pl.ds(g * HEAD_WIDTH, HEAD_WIDTH)
            values = acc[:, pl.ds(v_at + g * HEAD_WIDTH, HEAD_WIDTH)] * inverse
            blended = values + blend[:, g : g + 1] * earlier[:, kv_columns].astype(F32)
            mixed_values = jnp.where(is_first, values, blended).astype(BF16)
            key_high, key_low = split_high_low(
                unit_rows(acc[:, pl.ds(k_at + g * HEAD_WIDTH, HEAD_WIDTH)] * inverse)
            )
            keys = jnp.concatenate([key_high, key_high, key_low], axis=1)
            queries = []
            for j in range(group):
                h = g * group + j
                query_high, query_low = split_high_low(
                    unit_rows(acc[:, pl.ds(h * HEAD_WIDTH, HEAD_WIDTH)] * inverse)
                    * (scale[:, h : h + 1] / math.sqrt(HEAD_WIDTH))
                )
                queries.append(jnp.concatenate([query_high, query_low, query_high], axis=1))
            scores = lax.dot_general(
                jnp.concatenate(queries, axis=0),
                keys,
                (((1,), (1,)), ((), ())),
                preferred_element_type=F32,
            ).reshape(group, tokens, tokens)
            scores = jnp.where(allowed[None], scores, -1e30)
            exponent = jnp.exp(scores - jnp.max(scores, axis=-1, keepdims=True)).astype(BF16)
            result = dot(
                exponent.reshape(group * tokens, tokens),
                jnp.concatenate([mixed_values, mixed_ones], axis=1),
            )
            result = (result[:, :HEAD_WIDTH] / result[:, HEAD_WIDTH:]).astype(BF16)
            for j in range(group):
                att[me, :, pl.ds((g * group + j) * HEAD_WIDTH, HEAD_WIDTH)] = result[
                    j * tokens : (j + 1) * tokens
                ]
            columns = pl.ds(g * group * HEAD_WIDTH, group * HEAD_WIDTH)
            for step in range(1, heads):
                copy = remote(
                    att.at[me, :, columns],
                    att.at[me, :, columns],
                    a_send.at[turn, step - 1, g],
                    a_recv.at[turn, step - 1, g],
                    (section, replica, head_at(step)),
                )
                copy.start()
                a_copies.append((turn, copy))

    a_copies = []
    attend(section, f1, att1, 0, inverse1)

    def own_tile(att, c):
        rows = pl.ds(pl.multiple_of(me * q_width, q_width), q_width)
        columns = pl.ds(c * CHUNK, CHUNK)
        proj[:, columns] = dot(att[me], wo[rows, columns])

    def whole_tile(att, stream, c):
        columns = pl.ds(c * CHUNK, CHUNK)
        total = proj[:, columns] + stream[me, :, columns].astype(F32)
        for step in range(1, heads):
            peer = lax.rem(me + heads - step, heads)
            rows = pl.ds(pl.multiple_of(peer * q_width, q_width), q_width)
            total += dot(att[peer], wo[rows, columns])
        return total.astype(BF16)

    def z_copy(c):
        columns = pl.ds(c * CHUNK, CHUNK)
        return remote(
            out1.at[:, columns],
            x2.at[me, :, columns],
            z_send.at[c],
            z_recv.at[c],
            (section + 1, replica, me),
        )

    for load in wo_loads:
        load.wait()
    ahead = chunks // 2
    for c in range(ahead):
        own_tile(att1, c)
    for turn, copy in a_copies:
        if turn == 0:
            copy.wait_recv()
    for c in range(chunks):
        if c >= ahead:
            own_tile(att1, c)
        out1[:, pl.ds(c * CHUNK, CHUNK)] = whole_tile(att1, x1, c)

        @pl.when(not_last)
        def _(c=c):
            z_copy(c).start()

    out1_store = local(out1, out1_hbm.at[0], out_sem.at[0])

    def grad_part(turn, step):
        p = lax.rem(replica + replicas - step, replicas)
        return lax.dot_general(
            rows_n[turn, p],
            rows_c[p, turn],
            (((0,), (0,)), ((), ())),
            preferred_element_type=F32,
        )

    cot_load.wait()
    grad[...] = grad_part(0, 0)

    def forward(step, c):
        columns = pl.ds(c * CHUNK, CHUNK)
        return remote(
            x2.at[me, :, columns],
            x2.at[me, :, columns],
            f_send.at[step - 1, c],
            f_recv.at[step - 1, c],
            (section, replica, head_at(step)),
        )

    @pl.when(is_first)
    def _():
        for load in enter_loads:
            load.wait()

    squares = jnp.zeros((tokens, 1), F32)
    for c in range(chunks):
        columns = pl.ds(c * CHUNK, CHUNK)

        @pl.when(not_first)
        def _(c=c):
            z_copy(c).wait_recv()
            for step in range(1, heads):
                forward(step, c).start()

        part = x2[me, :, columns].astype(F32)
        squares += jnp.sum(part * part, axis=-1, keepdims=True)
        project(part, me * width + c * CHUNK, CHUNK, c == 0)
        if c < chunks - 1:
            for step in range(1 + c * (replicas - 1) // (chunks - 1), 1 + (c + 1) * (replicas - 1) // (chunks - 1)):
                c_copies[step - 1].wait_recv()
                n1_copies[step - 1].wait_recv()
                grad[...] += grad_part(0, step)

        @pl.when(not_first)
        def _(c=c):
            for step in range(1, heads):
                forward(step, c).wait_recv()

        parts = [x2[lax.rem(me + heads - step, heads), :, columns].astype(F32) for step in range(1, heads)]
        for part in parts:
            squares += jnp.sum(part * part, axis=-1, keepdims=True)
        if c == chunks - 1:
            inverse2 = normalize(x2, squares, normed2)
            n2_copies = send_normed(normed2, 1)
        for step in range(1, heads):
            owner = lax.rem(me + heads - step, heads)
            project(parts[step - 1], owner * width + c * CHUNK, CHUNK, False)

    @pl.when(not_first)
    def _():
        value_copy.wait_recv()

    attend(lax.rem(section + sections, sections + 1), f2, att2, 1, inverse2)
    for c in range(chunks):
        own_tile(att2, c)
    for turn, copy in a_copies:
        if turn == 1:
            copy.wait_recv()
    for c in range(chunks):
        out2[:, pl.ds(c * CHUNK, CHUNK)] = whole_tile(att2, x2, c)
    out2_store = local(out2, out2_hbm.at[0], out_sem.at[1])

    total = grad[...] + grad_part(1, 0)
    for step in range(1, replicas):
        n2_copies[step - 1].wait_recv()
        total += grad_part(1, step)
    grad[...] = total
    grad_store = local(grad, grad_hbm.at[0], out_sem.at[2])

    for copy in x_copies + c_copies + n1_copies + n2_copies:
        copy.wait_send()
    for _, copy in a_copies:
        copy.wait_send()

    @pl.when(not_last)
    def _():
        value_copy.wait_send()
        for c in range(chunks):
            z_copy(c).wait_send()

    @pl.when(not_first)
    def _():
        for c in range(chunks):
            for step in range(1, heads):
                forward(step, c).wait_send()

    out1_store.wait()
    out2_store.wait()
    grad_store.wait()


def store_kernel(*refs):
    sources, targets, buffers, load_sem, store_sem = refs[:3], refs[3:6], refs[6:9], refs[9], refs[10]
    loads, stores = [], []
    for source, target, buffer in zip(sources, targets, buffers):
        rows = source.shape[1] // STORE_BLOCKS
        for i in range(STORE_BLOCKS):
            block, n = pl.ds(i * rows, rows), len(loads)
            loads.append(
                pltpu.make_async_copy(source.at[0, block], buffer.at[block], load_sem.at[n])
            )
            stores.append(
                pltpu.make_async_copy(buffer.at[block], target.at[0, block], store_sem.at[n])
            )
    for load in loads:
        load.start()
    for load, store in zip(loads, stores):
        load.wait()
        store.start()
    for store in stores:
        store.wait()


def solution(mesh):
    sections, replicas, heads = (mesh.shape[a] for a in ("section", "dp", "head"))

    def per_device(
        segments,
        stream,
        entering,
        pending,
        gain,
        wq,
        wk,
        wv,
        wo,
        scale,
        blend,
        cotangent,
    ):
        _, tokens, width = stream.shape
        model = width * heads
        q_width, kv_width = wq.shape[2], wk.shape[2]
        grad_rows = model // replicas
        chunks = width // CHUNK
        kv_heads = kv_width // HEAD_WIDTH
        others = heads - 1
        peers = replicas - 1
        dma = pltpu.SemaphoreType.DMA
        scratch = [
            pltpu.VMEM(segments.shape, jnp.int32),
            pltpu.VMEM(gain.shape, F32),
            pltpu.VMEM(scale.shape, F32),
            pltpu.VMEM(blend.shape, F32),
            pltpu.VMEM((model, q_width), BF16),
            pltpu.VMEM((model, kv_width), BF16),
            pltpu.VMEM((model, kv_width), BF16),
            pltpu.VMEM((model, width), BF16),
            pltpu.VMEM((heads, tokens, width), BF16),
            pltpu.VMEM((heads, tokens, width), BF16),
            pltpu.VMEM((tokens, kv_width), BF16),
            pltpu.VMEM((tokens, kv_width), BF16),
            pltpu.VMEM((tokens, model), BF16),
            pltpu.VMEM((tokens, model), BF16),
            pltpu.VMEM((tokens, q_width + 2 * kv_width), F32),
            pltpu.VMEM((heads, tokens, q_width), BF16),
            pltpu.VMEM((heads, tokens, q_width), BF16),
            pltpu.VMEM((tokens, width), BF16),
            pltpu.VMEM((tokens, width), BF16),
            pltpu.VMEM((tokens, width), F32),
            pltpu.VMEM((2, replicas, tokens, grad_rows), BF16),
            pltpu.VMEM((replicas, 2, tokens, kv_width), BF16),
            pltpu.VMEM((grad_rows, kv_width), F32),
            dma((7,)),
            dma((4 * heads + 4,)),
            dma((heads,)),
            dma((3,)),
            dma((others,)),
            dma((others,)),
            dma((peers,)),
            dma((peers,)),
            dma((2, peers)),
            dma((2, peers)),
            dma((2, others, kv_heads)),
            dma((2, others, kv_heads)),
            dma((chunks,)),
            dma((chunks,)),
            dma((others, chunks)),
            dma((others, chunks)),
            dma((1,)),
            dma((1,)),
        ]
        results = pl.pallas_call(
            functools.partial(kernel, sections, replicas, heads),
            out_shape=(
                jax.ShapeDtypeStruct(stream.shape, BF16),
                jax.ShapeDtypeStruct(stream.shape, BF16),
                jax.ShapeDtypeStruct((1, grad_rows, kv_width), F32),
            ),
            in_specs=[pl.BlockSpec(memory_space=pl.ANY)] * 12,
            out_specs=(pl.BlockSpec(memory_space=pl.ANY),) * 3,
            scratch_shapes=scratch,
            compiler_params=pltpu.CompilerParams(
                collective_id=0, has_side_effects=True, vmem_limit_bytes=56 * 1024 * 1024
            ),
        )(
            segments,
            stream,
            entering,
            pending,
            gain,
            wq,
            wk,
            wv,
            wo,
            scale,
            blend,
            cotangent,
        )
        return pl.pallas_call(
            store_kernel,
            out_shape=tuple(jax.ShapeDtypeStruct(r.shape, r.dtype) for r in results),
            in_specs=[pl.BlockSpec(memory_space=pl.ANY)] * 3,
            out_specs=(pl.BlockSpec(memory_space=pl.ANY),) * 3,
            scratch_shapes=[pltpu.VMEM(r.shape[1:], r.dtype) for r in results]
            + [dma((3 * STORE_BLOCKS,)), dma((3 * STORE_BLOCKS,))],
            compiler_params=pltpu.CompilerParams(vmem_limit_bytes=56 * 1024 * 1024),
        )(*results)

    return jax.shard_map(
        per_device,
        mesh=mesh,
        in_specs=(
            P(None, "dp"),
            P("section", "dp", "head"),
            P("dp", None),
            P("section", "dp", "head"),
            P("section", None),
            P("section", None, "head"),
            P("section", None, "head"),
            P("section", None, "head"),
            P("section", None, "head"),
            P("section", "head"),
            P("section", "head"),
            P("section", None, "dp", "head"),
        ),
        out_specs=(
            P("section", "dp", "head"),
            P("section", "dp", "head"),
            P("section", "dp", "head"),
        ),
        check_vma=False,
    )
```

```python
import functools
import math

import jax
import jax.numpy as jnp
from jax import lax
from jax.experimental import pallas as pl
from jax.experimental.pallas import tpu as pltpu
from jax.sharding import PartitionSpec as P

HEAD_WIDTH = 128
CHUNK = 256
STORE_BLOCKS = 2
EPSILON = 1e-06
F32 = jnp.float32
BF16 = jnp.bfloat16


def dot(a, b):
    return jnp.dot(a, b, preferred_element_type=F32)


def split_high_low(values):
    high = values.astype(BF16)
    return high, (values - high.astype(F32)).astype(BF16)


def kernel(
    sections,
    replicas,
    heads,
    seg_hbm,
    x_hbm,
    entering_hbm,
    pending_hbm,
    gain_hbm,
    wq_hbm,
    wk_hbm,
    wv_hbm,
    wo_hbm,
    scale_hbm,
    blend_hbm,
    cot_hbm,
    out1_hbm,
    out2_hbm,
    grad_hbm,
    seg,
    gain,
    scale,
    blend,
    wq,
    wk,
    wv,
    wo,
    x1,
    x2,
    f1,
    f2,
    normed1,
    normed2,
    acc,
    att1,
    att2,
    out1,
    out2,
    proj,
    rows_n,
    rows_c,
    grad,
    local_sem,
    weight_sem,
    enter_sem,
    out_sem,
    x_send,
    x_recv,
    c_send,
    c_recv,
    n_send,
    n_recv,
    a_send,
    a_recv,
    z_send,
    z_recv,
    f_send,
    f_recv,
    v_send,
    v_recv,
):
    section = lax.axis_index("section")
    replica = lax.axis_index("dp")
    me = lax.axis_index("head")
    tokens, width = x1.shape[1], x1.shape[2]
    model = width * heads
    q_width, kv_width = wq.shape[1], wk.shape[1]
    kv_heads = kv_width // HEAD_WIDTH
    group = q_width // kv_width
    grad_rows = model // replicas
    chunks = width // CHUNK
    is_first = section == 0
    not_first = section > 0
    not_last = section < sections - 1

    def local(src, dst, sem):
        copy = pltpu.make_async_copy(src, dst, sem)
        copy.start()
        return copy

    def remote(src, dst, send, recv, where):
        return pltpu.make_async_remote_copy(
            src_ref=src,
            dst_ref=dst,
            send_sem=send,
            recv_sem=recv,
            device_id=where,
            device_id_type=pl.DeviceIdType.MESH,
        )

    def head_at(step):
        return lax.rem(me + step, heads)

    def replica_at(step):
        return lax.rem(replica + step, replicas)

    x_load = local(x_hbm.at[0], x1.at[me], local_sem.at[0])
    gain_load = local(gain_hbm, gain, local_sem.at[1])
    weight_loads = []
    for step in range(heads):
        first = pl.multiple_of(lax.rem(me + heads - step, heads) * width, CHUNK)
        half = width // 2
        blocks = [(wk_hbm, wk, first, width), (wv_hbm, wv, first, width)]
        blocks += [(wq_hbm, wq, first + i * half, half) for i in range(2)]
        weight_loads.append(
            [
                local(
                    source.at[0, pl.ds(pl.multiple_of(row, CHUNK), size)],
                    target.at[pl.ds(pl.multiple_of(row, CHUNK), size)],
                    weight_sem.at[4 * step + i],
                )
                for i, (source, target, row, size) in enumerate(blocks)
            ]
        )
    seg_load = local(seg_hbm, seg, local_sem.at[2])
    scale_load = local(scale_hbm, scale, local_sem.at[3])
    blend_load = local(blend_hbm, blend, local_sem.at[4])
    cot_load = local(cot_hbm.at[0], rows_c.at[replica], local_sem.at[5])
    f1_load = pltpu.make_async_copy(pending_hbm.at[0], f1, local_sem.at[6])

    @pl.when(not_first)
    def _():
        f1_load.start()

    quarter = model // 4
    wo_loads = [
        local(
            wo_hbm.at[0, pl.ds(i * quarter, quarter)],
            wo.at[pl.ds(i * quarter, quarter)],
            weight_sem.at[4 * heads + i],
        )
        for i in range(4)
    ]
    enter_loads = [
        pltpu.make_async_copy(
            entering_hbm.at[:, pl.ds(h * width, width)], x2.at[h], enter_sem.at[h]
        )
        for h in range(heads)
    ]

    @pl.when(is_first)
    def _():
        for load in enter_loads:
            load.start()
        f2[...] = jnp.zeros_like(f2)

    barrier = pltpu.get_barrier_semaphore()

    def greet(where):
        pl.semaphore_signal(barrier, inc=1, device_id=where, device_id_type=pl.DeviceIdType.MESH)

    for step in range(1, heads):
        greet((section, replica, head_at(step)))
    for step in range(1, replicas):
        greet((section, replica_at(step), me))

    @pl.when(not_first)
    def _():
        greet((section - 1, replica, me))

    @pl.when(not_last)
    def _():
        greet((section + 1, replica, me))

    pl.semaphore_wait(
        barrier,
        heads - 1 + replicas - 1 + not_first.astype(jnp.int32) + not_last.astype(jnp.int32),
    )

    x_copies = []
    for step in range(1, heads):
        copy = remote(
            x_hbm.at[0],
            x1.at[me],
            x_send.at[step - 1],
            x_recv.at[step - 1],
            (section, replica, head_at(step)),
        )
        copy.start()
        x_copies.append(copy)
    value_copy = remote(f1, f2, v_send.at[0], v_recv.at[0], (section + 1, replica, me))

    c_copies = []
    for step in range(1, replicas):
        copy = remote(
            cot_hbm.at[0],
            rows_c.at[replica],
            c_send.at[step - 1],
            c_recv.at[step - 1],
            (section, replica_at(step), me),
        )
        copy.start()
        c_copies.append(copy)

    k_at, v_at = q_width, q_width + kv_width
    weights_at = ((wk, k_at, kv_width), (wv, v_at, kv_width), (wq, 0, q_width))

    def project(pieces, size, is_start):
        scaled = []
        for part, first_row in pieces:
            rows = pl.ds(pl.multiple_of(first_row, CHUNK), size)
            scaled.append(((part * gain[:, rows]).astype(BF16), rows))
        for weight, at, columns in weights_at:
            product = dot(scaled[0][0], weight[scaled[0][1], :])
            for piece, rows in scaled[1:]:
                product += dot(piece, weight[rows, :])
            if is_start:
                acc[:, pl.ds(at, columns)] = product
            else:
                acc[:, pl.ds(at, columns)] += product

    def normalize(stream, squares, normed):
        inverse = lax.rsqrt(squares / model + EPSILON)
        for h in range(heads):
            columns = pl.ds(h * width, width)
            normed[:, columns] = (stream[h].astype(F32) * inverse * gain[:, columns]).astype(BF16)
        return inverse

    def send_normed(normed, turn):
        copies = []
        for step in range(1, replicas):
            peer = replica_at(step)
            first = pl.multiple_of(peer * grad_rows, 128)
            copy = remote(
                normed.at[:, pl.ds(first, grad_rows)],
                rows_n.at[turn, replica],
                n_send.at[turn, step - 1],
                n_recv.at[turn, step - 1],
                (section, peer, me),
            )
            copy.start()
            copies.append(copy)
        first = pl.multiple_of(replica * grad_rows, 128)
        rows_n[turn, replica] = normed[:, pl.ds(first, grad_rows)]
        return copies

    gain_load.wait()
    x_load.wait()
    for load in weight_loads[0]:
        load.wait()
    part = x1[me].astype(F32)
    squares = jnp.sum(part * part, axis=-1, keepdims=True)
    project([(part, me * width)], width, True)
    for copy in x_copies:
        copy.wait_recv()
    for step in range(1, heads):
        part = x1[lax.rem(me + heads - step, heads)].astype(F32)
        squares += jnp.sum(part * part, axis=-1, keepdims=True)
    inverse1 = normalize(x1, squares, normed1)
    n1_copies = send_normed(normed1, 0)
    for step in range(1, heads):
        for load in weight_loads[step]:
            load.wait()
        owner = lax.rem(me + heads - step, heads)
        project([(x1[owner].astype(F32), owner * width)], width, False)

    seg_load.wait()
    scale_load.wait()
    blend_load.wait()

    @pl.when(not_first)
    def _():
        f1_load.wait()

    @pl.when(is_first)
    def _():
        f1[...] = (acc[:, pl.ds(v_at, kv_width)] * inverse1).astype(BF16)

    @pl.when(not_last)
    def _():
        value_copy.start()

    causal = lax.broadcasted_iota(jnp.int32, (tokens, tokens), 0) >= lax.broadcasted_iota(
        jnp.int32, (tokens, tokens), 1
    )

    ones = jnp.ones((2 * HEAD_WIDTH, HEAD_WIDTH), BF16)
    mixed_ones = jnp.ones((tokens, HEAD_WIDTH), BF16)

    def unit_rows(values):
        total = dot(jnp.concatenate(split_high_low(values * values), axis=1), ones)
        return values * lax.rsqrt(total / HEAD_WIDTH + EPSILON)

    def attend(segment_index, earlier, att, turn, inverse):
        row = seg[pl.ds(segment_index, 1), :].astype(F32)
        across = jnp.broadcast_to(row, (tokens, tokens))
        allowed = causal & (across == across.T)
        queries, keys, mixes = [], [], []
        for g in range(kv_heads):
            kv_columns = pl.ds(g * HEAD_WIDTH, HEAD_WIDTH)
            values = acc[:, pl.ds(v_at + g * HEAD_WIDTH, HEAD_WIDTH)] * inverse
            blended = values + blend[:, g : g + 1] * earlier[:, kv_columns].astype(F32)
            mixed_values = jnp.where(is_first, values, blended).astype(BF16)
            mixes.append(jnp.concatenate([mixed_values, mixed_ones], axis=1))
            stacked = [acc[:, pl.ds(k_at + g * HEAD_WIDTH, HEAD_WIDTH)] * inverse]
            for h in range(g * group, (g + 1) * group):
                stacked.append(acc[:, pl.ds(h * HEAD_WIDTH, HEAD_WIDTH)] * inverse)
            unit = unit_rows(jnp.concatenate(stacked, axis=0))
            key_high, key_low = split_high_low(unit[:tokens])
            keys.append(jnp.concatenate([key_high, key_high, key_low], axis=1))
            parts = []
            for j in range(group):
                h = g * group + j
                query_high, query_low = split_high_low(
                    unit[(j + 1) * tokens : (j + 2) * tokens]
                    * (scale[:, h : h + 1] / math.sqrt(HEAD_WIDTH))
                )
                parts.append(jnp.concatenate([query_high, query_low, query_high], axis=1))
            queries.append(jnp.concatenate(parts, axis=0))
        scores = [
            lax.dot_general(q, k, (((1,), (1,)), ((), ())), preferred_element_type=F32)
            for q, k in zip(queries, keys)
        ]
        exponents = []
        for score in scores:
            score = jnp.where(allowed[None], score.reshape(group, tokens, tokens), -1e30)
            top = jnp.max(score, axis=-1, keepdims=True)
            exponents.append(jnp.exp(score - top).astype(BF16).reshape(group * tokens, tokens))
        results = [dot(e, m) for e, m in zip(exponents, mixes)]
        for g, result in enumerate(results):
            result = (result[:, :HEAD_WIDTH] / result[:, HEAD_WIDTH:]).astype(BF16)
            for j in range(group):
                att[me, :, pl.ds((g * group + j) * HEAD_WIDTH, HEAD_WIDTH)] = result[
                    j * tokens : (j + 1) * tokens
                ]
        for step in range(1, heads):
            copy = remote(
                att.at[me],
                att.at[me],
                a_send.at[turn, step - 1],
                a_recv.at[turn, step - 1],
                (section, replica, head_at(step)),
            )
            copy.start()
            a_copies.append((turn, copy))

    a_copies = []
    attend(section, f1, att1, 0, inverse1)

    def own_tile(att, c):
        rows = pl.ds(pl.multiple_of(me * q_width, q_width), q_width)
        columns = pl.ds(c * CHUNK, CHUNK)
        proj[:, columns] = dot(att[me], wo[rows, columns])

    def whole_tile(att, stream, c):
        columns = pl.ds(c * CHUNK, CHUNK)
        total = proj[:, columns] + stream[me, :, columns].astype(F32)
        for step in range(1, heads):
            peer = lax.rem(me + heads - step, heads)
            rows = pl.ds(pl.multiple_of(peer * q_width, q_width), q_width)
            total += dot(att[peer], wo[rows, columns])
        return total.astype(BF16)

    def z_copy(c):
        columns = pl.ds(c * CHUNK, CHUNK)
        return remote(
            out1.at[:, columns],
            x2.at[me, :, columns],
            z_send.at[c],
            z_recv.at[c],
            (section + 1, replica, me),
        )

    for load in wo_loads:
        load.wait()
    ahead = chunks // 2
    for c in range(ahead):
        own_tile(att1, c)
    for turn, copy in a_copies:
        if turn == 0:
            copy.wait_recv()
    for c in range(chunks):
        if c >= ahead:
            own_tile(att1, c)
        out1[:, pl.ds(c * CHUNK, CHUNK)] = whole_tile(att1, x1, c)

        @pl.when(not_last)
        def _(c=c):
            z_copy(c).start()

    out1_store = local(out1, out1_hbm.at[0], out_sem.at[0])

    def grad_part(turn):
        features = jnp.concatenate([rows_n[turn, p] for p in range(replicas)], axis=0)
        cotangents = jnp.concatenate([rows_c[p, turn] for p in range(replicas)], axis=0)
        return lax.dot_general(
            features, cotangents, (((0,), (0,)), ((), ())), preferred_element_type=F32
        )

    cot_load.wait()

    def forward(step, c):
        columns = pl.ds(c * CHUNK, CHUNK)
        return remote(
            x2.at[me, :, columns],
            x2.at[me, :, columns],
            f_send.at[step - 1, c],
            f_recv.at[step - 1, c],
            (section, replica, head_at(step)),
        )

    @pl.when(is_first)
    def _():
        for load in enter_loads:
            load.wait()

    squares = jnp.zeros((tokens, 1), F32)
    for c in range(chunks + 1):
        @pl.when(not_first)
        def _(c=c):
            if c < chunks:
                z_copy(c).wait_recv()
                for step in range(1, heads):
                    forward(step, c).start()
            if c > 0:
                for step in range(1, heads):
                    forward(step, c - 1).wait_recv()

        pieces = []
        for step in range(heads):
            at = c if step == 0 else c - 1
            if 0 <= at < chunks:
                owner = lax.rem(me + heads - step, heads)
                part = x2[owner, :, pl.ds(at * CHUNK, CHUNK)].astype(F32)
                squares += jnp.sum(part * part, axis=-1, keepdims=True)
                pieces.append((part, owner * width + at * CHUNK))
        if c == chunks:
            inverse2 = normalize(x2, squares, normed2)
            n2_copies = send_normed(normed2, 1)
        project(pieces, CHUNK, c == 0)
        if c == chunks - 2:
            for copy in c_copies + n1_copies:
                copy.wait_recv()
            grad[...] = grad_part(0)

    @pl.when(not_first)
    def _():
        value_copy.wait_recv()

    attend(lax.rem(section + sections, sections + 1), f2, att2, 1, inverse2)
    for c in range(chunks):
        own_tile(att2, c)
    for turn, copy in a_copies:
        if turn == 1:
            copy.wait_recv()
    for c in range(chunks):
        out2[:, pl.ds(c * CHUNK, CHUNK)] = whole_tile(att2, x2, c)
    out2_store = local(out2, out2_hbm.at[0], out_sem.at[1])

    for copy in n2_copies:
        copy.wait_recv()
    grad[...] += grad_part(1)
    grad_store = local(grad, grad_hbm.at[0], out_sem.at[2])

    for copy in x_copies + c_copies + n1_copies + n2_copies:
        copy.wait_send()
    for _, copy in a_copies:
        copy.wait_send()

    @pl.when(not_last)
    def _():
        value_copy.wait_send()
        for c in range(chunks):
            z_copy(c).wait_send()

    @pl.when(not_first)
    def _():
        for c in range(chunks):
            for step in range(1, heads):
                forward(step, c).wait_send()

    out1_store.wait()
    out2_store.wait()
    grad_store.wait()


def store_kernel(*refs):
    sources, targets, buffers, load_sem, store_sem = refs[:3], refs[3:6], refs[6:9], refs[9], refs[10]
    loads, stores = [], []
    for source, target, buffer in zip(sources, targets, buffers):
        rows = source.shape[1] // STORE_BLOCKS
        for i in range(STORE_BLOCKS):
            block, n = pl.ds(i * rows, rows), len(loads)
            loads.append(
                pltpu.make_async_copy(source.at[0, block], buffer.at[block], load_sem.at[n])
            )
            stores.append(
                pltpu.make_async_copy(buffer.at[block], target.at[0, block], store_sem.at[n])
            )
    for load in loads:
        load.start()
    for load, store in zip(loads, stores):
        load.wait()
        store.start()
    for store in stores:
        store.wait()


def solution(mesh):
    sections, replicas, heads = (mesh.shape[a] for a in ("section", "dp", "head"))

    def per_device(
        segments,
        stream,
        entering,
        pending,
        gain,
        wq,
        wk,
        wv,
        wo,
        scale,
        blend,
        cotangent,
    ):
        _, tokens, width = stream.shape
        model = width * heads
        q_width, kv_width = wq.shape[2], wk.shape[2]
        grad_rows = model // replicas
        chunks = width // CHUNK
        others = heads - 1
        peers = replicas - 1
        dma = pltpu.SemaphoreType.DMA
        scratch = [
            pltpu.VMEM(segments.shape, jnp.int32),
            pltpu.VMEM(gain.shape, F32),
            pltpu.VMEM(scale.shape, F32),
            pltpu.VMEM(blend.shape, F32),
            pltpu.VMEM((model, q_width), BF16),
            pltpu.VMEM((model, kv_width), BF16),
            pltpu.VMEM((model, kv_width), BF16),
            pltpu.VMEM((model, width), BF16),
            pltpu.VMEM((heads, tokens, width), BF16),
            pltpu.VMEM((heads, tokens, width), BF16),
            pltpu.VMEM((tokens, kv_width), BF16),
            pltpu.VMEM((tokens, kv_width), BF16),
            pltpu.VMEM((tokens, model), BF16),
            pltpu.VMEM((tokens, model), BF16),
            pltpu.VMEM((tokens, q_width + 2 * kv_width), F32),
            pltpu.VMEM((heads, tokens, q_width), BF16),
            pltpu.VMEM((heads, tokens, q_width), BF16),
            pltpu.VMEM((tokens, width), BF16),
            pltpu.VMEM((tokens, width), BF16),
            pltpu.VMEM((tokens, width), F32),
            pltpu.VMEM((2, replicas, tokens, grad_rows), BF16),
            pltpu.VMEM((replicas, 2, tokens, kv_width), BF16),
            pltpu.VMEM((grad_rows, kv_width), F32),
            dma((7,)),
            dma((4 * heads + 4,)),
            dma((heads,)),
            dma((3,)),
            dma((others,)),
            dma((others,)),
            dma((peers,)),
            dma((peers,)),
            dma((2, peers)),
            dma((2, peers)),
            dma((2, others)),
            dma((2, others)),
            dma((chunks,)),
            dma((chunks,)),
            dma((others, chunks)),
            dma((others, chunks)),
            dma((1,)),
            dma((1,)),
        ]
        results = pl.pallas_call(
            functools.partial(kernel, sections, replicas, heads),
            out_shape=(
                jax.ShapeDtypeStruct(stream.shape, BF16),
                jax.ShapeDtypeStruct(stream.shape, BF16),
                jax.ShapeDtypeStruct((1, grad_rows, kv_width), F32),
            ),
            in_specs=[pl.BlockSpec(memory_space=pl.ANY)] * 12,
            out_specs=(pl.BlockSpec(memory_space=pl.ANY),) * 3,
            scratch_shapes=scratch,
            compiler_params=pltpu.CompilerParams(
                collective_id=0, has_side_effects=True, vmem_limit_bytes=56 * 1024 * 1024
            ),
        )(
            segments,
            stream,
            entering,
            pending,
            gain,
            wq,
            wk,
            wv,
            wo,
            scale,
            blend,
            cotangent,
        )
        return pl.pallas_call(
            store_kernel,
            out_shape=tuple(jax.ShapeDtypeStruct(r.shape, r.dtype) for r in results),
            in_specs=[pl.BlockSpec(memory_space=pl.ANY)] * 3,
            out_specs=(pl.BlockSpec(memory_space=pl.ANY),) * 3,
            scratch_shapes=[pltpu.VMEM(r.shape[1:], r.dtype) for r in results]
            + [dma((3 * STORE_BLOCKS,)), dma((3 * STORE_BLOCKS,))],
            compiler_params=pltpu.CompilerParams(vmem_limit_bytes=56 * 1024 * 1024),
        )(*results)

    return jax.shard_map(
        per_device,
        mesh=mesh,
        in_specs=(
            P(None, "dp"),
            P("section", "dp", "head"),
            P("dp", None),
            P("section", "dp", "head"),
            P("section", None),
            P("section", None, "head"),
            P("section", None, "head"),
            P("section", None, "head"),
            P("section", None, "head"),
            P("section", "head"),
            P("section", "head"),
            P("section", None, "dp", "head"),
        ),
        out_specs=(
            P("section", "dp", "head"),
            P("section", "dp", "head"),
            P("section", "dp", "head"),
        ),
        check_vma=False,
    )
```

```python
import functools
import math

import jax
import jax.numpy as jnp
from jax import lax
from jax.experimental import pallas as pl
from jax.experimental.pallas import tpu as pltpu
from jax.sharding import PartitionSpec as P

HEAD_WIDTH = 128
CHUNK = 256
STORE_BLOCKS = 2
EPSILON = 1e-06
F32 = jnp.float32
BF16 = jnp.bfloat16


def dot(a, b):
    return jnp.dot(a, b, preferred_element_type=F32)


def split_high_low(values):
    high = values.astype(BF16)
    return high, (values - high.astype(F32)).astype(BF16)


def kernel(
    sections,
    replicas,
    heads,
    seg_hbm,
    x_hbm,
    entering_hbm,
    pending_hbm,
    gain_hbm,
    wq_hbm,
    wk_hbm,
    wv_hbm,
    wo_hbm,
    scale_hbm,
    blend_hbm,
    cot_hbm,
    out1_hbm,
    out2_hbm,
    grad_hbm,
    seg,
    gain,
    scale,
    blend,
    wq,
    wk,
    wv,
    wo,
    x1,
    x2,
    f1,
    f2,
    normed1,
    normed2,
    acc,
    att1,
    att2,
    out1,
    out2,
    proj,
    rows_n,
    rows_c,
    grad,
    local_sem,
    weight_sem,
    enter_sem,
    out_sem,
    x_send,
    x_recv,
    c_send,
    c_recv,
    n_send,
    n_recv,
    a_send,
    a_recv,
    z_send,
    z_recv,
    f_send,
    f_recv,
    v_send,
    v_recv,
    h_send,
    h_recv,
):
    section = lax.axis_index("section")
    replica = lax.axis_index("dp")
    me = lax.axis_index("head")
    tokens, width = x1.shape[1], x1.shape[2]
    model = width * heads
    q_width, kv_width = wq.shape[1], wk.shape[1]
    kv_heads = kv_width // HEAD_WIDTH
    group = q_width // kv_width
    grad_rows = model // replicas
    chunks = width // CHUNK
    is_first = section == 0
    not_first = section > 0
    not_last = section < sections - 1

    def local(src, dst, sem):
        copy = pltpu.make_async_copy(src, dst, sem)
        copy.start()
        return copy

    def remote(src, dst, send, recv, where):
        return pltpu.make_async_remote_copy(
            src_ref=src,
            dst_ref=dst,
            send_sem=send,
            recv_sem=recv,
            device_id=where,
            device_id_type=pl.DeviceIdType.MESH,
        )

    def head_at(step):
        return lax.rem(me + step, heads)

    def replica_at(step):
        return lax.rem(replica + step, replicas)

    x_load = local(x_hbm.at[0], x1.at[me], local_sem.at[0])
    gain_load = local(gain_hbm, gain, local_sem.at[1])
    weight_loads = []
    for step in range(heads):
        first = pl.multiple_of(lax.rem(me + heads - step, heads) * width, CHUNK)
        half = width // 2
        blocks = [(wk_hbm, wk, first, width), (wv_hbm, wv, first, width)]
        blocks += [(wq_hbm, wq, first + i * half, half) for i in range(2)]
        weight_loads.append(
            [
                local(
                    source.at[0, pl.ds(pl.multiple_of(row, CHUNK), size)],
                    target.at[pl.ds(pl.multiple_of(row, CHUNK), size)],
                    weight_sem.at[4 * step + i],
                )
                for i, (source, target, row, size) in enumerate(blocks)
            ]
        )
    seg_load = local(seg_hbm, seg, local_sem.at[2])
    scale_load = local(scale_hbm, scale, local_sem.at[3])
    blend_load = local(blend_hbm, blend, local_sem.at[4])
    cot_load = local(cot_hbm.at[0], rows_c.at[replica], local_sem.at[5])
    f1_load = pltpu.make_async_copy(pending_hbm.at[0], f1, local_sem.at[6])

    @pl.when(not_first)
    def _():
        f1_load.start()

    quarter = model // 4
    wo_loads = [
        local(
            wo_hbm.at[0, pl.ds(i * quarter, quarter)],
            wo.at[pl.ds(i * quarter, quarter)],
            weight_sem.at[4 * heads + i],
        )
        for i in range(4)
    ]
    enter_loads = [
        pltpu.make_async_copy(
            entering_hbm.at[:, pl.ds(h * width, width)], x2.at[h], enter_sem.at[h]
        )
        for h in range(heads)
    ]

    @pl.when(is_first)
    def _():
        for load in enter_loads:
            load.start()
        f2[...] = jnp.zeros_like(f2)

    barrier = pltpu.get_barrier_semaphore()

    def greet(where):
        pl.semaphore_signal(barrier, inc=1, device_id=where, device_id_type=pl.DeviceIdType.MESH)

    for step in range(1, heads):
        greet((section, replica, head_at(step)))
    for step in range(1, replicas):
        greet((section, replica_at(step), me))

    @pl.when(not_first)
    def _():
        greet((section - 1, replica, me))

    @pl.when(not_last)
    def _():
        greet((section + 1, replica, me))

    pl.semaphore_wait(
        barrier,
        heads - 1 + replicas - 1 + not_first.astype(jnp.int32) + not_last.astype(jnp.int32),
    )

    x_copies = []
    for step in range(1, heads):
        copy = remote(
            x_hbm.at[0],
            x1.at[me],
            x_send.at[step - 1],
            x_recv.at[step - 1],
            (section, replica, head_at(step)),
        )
        copy.start()
        x_copies.append(copy)
    value_copy = remote(f1, f2, v_send.at[0], v_recv.at[0], (section + 1, replica, me))

    c_copies = []
    for step in range(1, replicas):
        copy = remote(
            cot_hbm.at[0],
            rows_c.at[replica],
            c_send.at[step - 1],
            c_recv.at[step - 1],
            (section, replica_at(step), me),
        )
        copy.start()
        c_copies.append(copy)

    k_at, v_at = q_width, q_width + kv_width
    weights_at = ((wk, k_at, kv_width), (wv, v_at, kv_width), (wq, 0, q_width))

    def project(pieces, size, is_start):
        scaled = []
        for part, first_row in pieces:
            rows = pl.ds(pl.multiple_of(first_row, CHUNK), size)
            scaled.append(((part * gain[:, rows]).astype(BF16), rows))
        for weight, at, columns in weights_at:
            product = dot(scaled[0][0], weight[scaled[0][1], :])
            for piece, rows in scaled[1:]:
                product += dot(piece, weight[rows, :])
            if is_start:
                acc[:, pl.ds(at, columns)] = product
            else:
                acc[:, pl.ds(at, columns)] += product

    def normalize(stream, squares, normed):
        inverse = lax.rsqrt(squares / model + EPSILON)
        for h in range(heads):
            columns = pl.ds(h * width, width)
            normed[:, columns] = (stream[h].astype(F32) * inverse * gain[:, columns]).astype(BF16)
        return inverse

    share_rows = tokens // heads
    share = pl.ds(pl.multiple_of(me * share_rows, share_rows), share_rows)

    def hand_on(copies, turn):
        handed = []
        for step in range(1, replicas):
            copies[step - 1].wait_recv()
            block = rows_n.at[turn, lax.rem(replica + replicas - step, replicas), share]
            for hop in range(1, heads):
                copy = remote(
                    block,
                    block,
                    h_send.at[turn, step - 1, hop - 1],
                    h_recv.at[turn, step - 1, hop - 1],
                    (section, replica, head_at(hop)),
                )
                copy.start()
                handed.append(copy)
        return handed

    def send_normed(normed, turn):
        copies = []
        for step in range(1, replicas):
            peer = replica_at(step)
            first = pl.multiple_of(peer * grad_rows, 128)
            copy = remote(
                normed.at[share, pl.ds(first, grad_rows)],
                rows_n.at[turn, replica, share],
                n_send.at[turn, step - 1],
                n_recv.at[turn, step - 1],
                (section, peer, me),
            )
            copy.start()
            copies.append(copy)
        first = pl.multiple_of(replica * grad_rows, 128)
        rows_n[turn, replica] = normed[:, pl.ds(first, grad_rows)]
        return copies

    gain_load.wait()
    x_load.wait()
    for load in weight_loads[0]:
        load.wait()
    part = x1[me].astype(F32)
    squares = jnp.sum(part * part, axis=-1, keepdims=True)
    project([(part, me * width)], width, True)
    for copy in x_copies:
        copy.wait_recv()
    for step in range(1, heads):
        part = x1[lax.rem(me + heads - step, heads)].astype(F32)
        squares += jnp.sum(part * part, axis=-1, keepdims=True)
    inverse1 = normalize(x1, squares, normed1)
    n1_copies = send_normed(normed1, 0)
    for step in range(1, heads):
        for load in weight_loads[step]:
            load.wait()
        owner = lax.rem(me + heads - step, heads)
        project([(x1[owner].astype(F32), owner * width)], width, False)

    seg_load.wait()
    scale_load.wait()
    blend_load.wait()

    @pl.when(not_first)
    def _():
        f1_load.wait()

    @pl.when(is_first)
    def _():
        f1[...] = (acc[:, pl.ds(v_at, kv_width)] * inverse1).astype(BF16)

    @pl.when(not_last)
    def _():
        value_copy.start()

    causal = lax.broadcasted_iota(jnp.int32, (tokens, tokens), 0) >= lax.broadcasted_iota(
        jnp.int32, (tokens, tokens), 1
    )

    ones = jnp.ones((2 * HEAD_WIDTH, HEAD_WIDTH), BF16)
    mixed_ones = jnp.ones((tokens, HEAD_WIDTH), BF16)

    def unit_rows(values):
        total = dot(jnp.concatenate(split_high_low(values * values), axis=1), ones)
        return values * lax.rsqrt(total / HEAD_WIDTH + EPSILON)

    def attend(segment_index, earlier, att, turn, inverse):
        row = seg[pl.ds(segment_index, 1), :].astype(F32)
        across = jnp.broadcast_to(row, (tokens, tokens))
        allowed = causal & (across == across.T)
        queries, keys, mixes = [], [], []
        for g in range(kv_heads):
            kv_columns = pl.ds(g * HEAD_WIDTH, HEAD_WIDTH)
            values = acc[:, pl.ds(v_at + g * HEAD_WIDTH, HEAD_WIDTH)] * inverse
            blended = values + blend[:, g : g + 1] * earlier[:, kv_columns].astype(F32)
            mixed_values = jnp.where(is_first, values, blended).astype(BF16)
            mixes.append(jnp.concatenate([mixed_values, mixed_ones], axis=1))
            stacked = [acc[:, pl.ds(k_at + g * HEAD_WIDTH, HEAD_WIDTH)] * inverse]
            for h in range(g * group, (g + 1) * group):
                stacked.append(acc[:, pl.ds(h * HEAD_WIDTH, HEAD_WIDTH)] * inverse)
            unit = unit_rows(jnp.concatenate(stacked, axis=0))
            key_high, key_low = split_high_low(unit[:tokens])
            keys.append(jnp.concatenate([key_high, key_high, key_low], axis=1))
            parts = []
            for j in range(group):
                h = g * group + j
                query_high, query_low = split_high_low(
                    unit[(j + 1) * tokens : (j + 2) * tokens]
                    * (scale[:, h : h + 1] / math.sqrt(HEAD_WIDTH))
                )
                parts.append(jnp.concatenate([query_high, query_low, query_high], axis=1))
            queries.append(jnp.concatenate(parts, axis=0))
        scores = [
            lax.dot_general(q, k, (((1,), (1,)), ((), ())), preferred_element_type=F32)
            for q, k in zip(queries, keys)
        ]
        exponents = []
        for score in scores:
            score = jnp.where(allowed[None], score.reshape(group, tokens, tokens), -1e30)
            top = jnp.max(score, axis=-1, keepdims=True)
            exponents.append(jnp.exp(score - top).astype(BF16).reshape(group * tokens, tokens))
        results = [dot(e, m) for e, m in zip(exponents, mixes)]
        for g, result in enumerate(results):
            result = (result[:, :HEAD_WIDTH] / result[:, HEAD_WIDTH:]).astype(BF16)
            for j in range(group):
                att[me, :, pl.ds((g * group + j) * HEAD_WIDTH, HEAD_WIDTH)] = result[
                    j * tokens : (j + 1) * tokens
                ]
        for step in range(1, heads):
            copy = remote(
                att.at[me],
                att.at[me],
                a_send.at[turn, step - 1],
                a_recv.at[turn, step - 1],
                (section, replica, head_at(step)),
            )
            copy.start()
            a_copies.append((turn, copy))

    a_copies = []
    attend(section, f1, att1, 0, inverse1)

    def own_tile(att, c):
        rows = pl.ds(pl.multiple_of(me * q_width, q_width), q_width)
        columns = pl.ds(c * CHUNK, CHUNK)
        proj[:, columns] = dot(att[me], wo[rows, columns])

    def whole_tile(att, stream, c):
        columns = pl.ds(c * CHUNK, CHUNK)
        total = proj[:, columns] + stream[me, :, columns].astype(F32)
        for step in range(1, heads):
            peer = lax.rem(me + heads - step, heads)
            rows = pl.ds(pl.multiple_of(peer * q_width, q_width), q_width)
            total += dot(att[peer], wo[rows, columns])
        return total.astype(BF16)

    def z_copy(c):
        columns = pl.ds(c * CHUNK, CHUNK)
        return remote(
            out1.at[:, columns],
            x2.at[me, :, columns],
            z_send.at[c],
            z_recv.at[c],
            (section + 1, replica, me),
        )

    for load in wo_loads:
        load.wait()
    ahead = chunks // 2
    for c in range(ahead):
        own_tile(att1, c)
    for turn, copy in a_copies:
        if turn == 0:
            copy.wait_recv()
    for c in range(chunks):
        if c >= ahead:
            own_tile(att1, c)
        out1[:, pl.ds(c * CHUNK, CHUNK)] = whole_tile(att1, x1, c)

        @pl.when(not_last)
        def _(c=c):
            z_copy(c).start()

    out1_store = local(out1, out1_hbm.at[0], out_sem.at[0])

    def grad_part(turn):
        features = jnp.concatenate([rows_n[turn, p] for p in range(replicas)], axis=0)
        cotangents = jnp.concatenate([rows_c[p, turn] for p in range(replicas)], axis=0)
        return lax.dot_general(
            features, cotangents, (((0,), (0,)), ((), ())), preferred_element_type=F32
        )

    cot_load.wait()

    def forward(step, c):
        columns = pl.ds(c * CHUNK, CHUNK)
        return remote(
            x2.at[me, :, columns],
            x2.at[me, :, columns],
            f_send.at[step - 1, c],
            f_recv.at[step - 1, c],
            (section, replica, head_at(step)),
        )

    @pl.when(is_first)
    def _():
        for load in enter_loads:
            load.wait()

    squares = jnp.zeros((tokens, 1), F32)
    for c in range(chunks + 1):
        @pl.when(not_first)
        def _(c=c):
            if c < chunks:
                z_copy(c).wait_recv()
                for step in range(1, heads):
                    forward(step, c).start()
            if c > 0:
                for step in range(1, heads):
                    forward(step, c - 1).wait_recv()

        pieces = []
        for step in range(heads):
            at = c if step == 0 else c - 1
            if 0 <= at < chunks:
                owner = lax.rem(me + heads - step, heads)
                part = x2[owner, :, pl.ds(at * CHUNK, CHUNK)].astype(F32)
                squares += jnp.sum(part * part, axis=-1, keepdims=True)
                pieces.append((part, owner * width + at * CHUNK))
        if c == chunks:
            inverse2 = normalize(x2, squares, normed2)
            n2_copies = send_normed(normed2, 1)
        project(pieces, CHUNK, c == 0)
        if c == chunks - 2:
            handed1 = hand_on(n1_copies, 0)
        if c == chunks - 1:
            for copy in c_copies + handed1:
                copy.wait_recv()
            grad[...] = grad_part(0)

    @pl.when(not_first)
    def _():
        value_copy.wait_recv()

    attend(lax.rem(section + sections, sections + 1), f2, att2, 1, inverse2)
    for c in range(chunks):
        own_tile(att2, c)
    for turn, copy in a_copies:
        if turn == 1:
            copy.wait_recv()
    for c in range(chunks):
        if c == chunks // 2:
            handed2 = hand_on(n2_copies, 1)
        out2[:, pl.ds(c * CHUNK, CHUNK)] = whole_tile(att2, x2, c)
    out2_store = local(out2, out2_hbm.at[0], out_sem.at[1])

    for copy in handed2:
        copy.wait_recv()
    grad[...] += grad_part(1)
    grad_store = local(grad, grad_hbm.at[0], out_sem.at[2])

    for copy in x_copies + c_copies + n1_copies + n2_copies + handed1 + handed2:
        copy.wait_send()
    for _, copy in a_copies:
        copy.wait_send()

    @pl.when(not_last)
    def _():
        value_copy.wait_send()
        for c in range(chunks):
            z_copy(c).wait_send()

    @pl.when(not_first)
    def _():
        for c in range(chunks):
            for step in range(1, heads):
                forward(step, c).wait_send()

    out1_store.wait()
    out2_store.wait()
    grad_store.wait()


def store_kernel(*refs):
    sources, targets, buffers, load_sem, store_sem = refs[:3], refs[3:6], refs[6:9], refs[9], refs[10]
    loads, stores = [], []
    for source, target, buffer in zip(sources, targets, buffers):
        rows = source.shape[1] // STORE_BLOCKS
        for i in range(STORE_BLOCKS):
            block, n = pl.ds(i * rows, rows), len(loads)
            loads.append(
                pltpu.make_async_copy(source.at[0, block], buffer.at[block], load_sem.at[n])
            )
            stores.append(
                pltpu.make_async_copy(buffer.at[block], target.at[0, block], store_sem.at[n])
            )
    for load in loads:
        load.start()
    for load, store in zip(loads, stores):
        load.wait()
        store.start()
    for store in stores:
        store.wait()


def solution(mesh):
    sections, replicas, heads = (mesh.shape[a] for a in ("section", "dp", "head"))

    def per_device(
        segments,
        stream,
        entering,
        pending,
        gain,
        wq,
        wk,
        wv,
        wo,
        scale,
        blend,
        cotangent,
    ):
        _, tokens, width = stream.shape
        model = width * heads
        q_width, kv_width = wq.shape[2], wk.shape[2]
        grad_rows = model // replicas
        chunks = width // CHUNK
        others = heads - 1
        peers = replicas - 1
        dma = pltpu.SemaphoreType.DMA
        scratch = [
            pltpu.VMEM(segments.shape, jnp.int32),
            pltpu.VMEM(gain.shape, F32),
            pltpu.VMEM(scale.shape, F32),
            pltpu.VMEM(blend.shape, F32),
            pltpu.VMEM((model, q_width), BF16),
            pltpu.VMEM((model, kv_width), BF16),
            pltpu.VMEM((model, kv_width), BF16),
            pltpu.VMEM((model, width), BF16),
            pltpu.VMEM((heads, tokens, width), BF16),
            pltpu.VMEM((heads, tokens, width), BF16),
            pltpu.VMEM((tokens, kv_width), BF16),
            pltpu.VMEM((tokens, kv_width), BF16),
            pltpu.VMEM((tokens, model), BF16),
            pltpu.VMEM((tokens, model), BF16),
            pltpu.VMEM((tokens, q_width + 2 * kv_width), F32),
            pltpu.VMEM((heads, tokens, q_width), BF16),
            pltpu.VMEM((heads, tokens, q_width), BF16),
            pltpu.VMEM((tokens, width), BF16),
            pltpu.VMEM((tokens, width), BF16),
            pltpu.VMEM((tokens, width), F32),
            pltpu.VMEM((2, replicas, tokens, grad_rows), BF16),
            pltpu.VMEM((replicas, 2, tokens, kv_width), BF16),
            pltpu.VMEM((grad_rows, kv_width), F32),
            dma((7,)),
            dma((4 * heads + 4,)),
            dma((heads,)),
            dma((3,)),
            dma((others,)),
            dma((others,)),
            dma((peers,)),
            dma((peers,)),
            dma((2, peers)),
            dma((2, peers)),
            dma((2, others)),
            dma((2, others)),
            dma((chunks,)),
            dma((chunks,)),
            dma((others, chunks)),
            dma((others, chunks)),
            dma((1,)),
            dma((1,)),
            dma((2, peers, others)),
            dma((2, peers, others)),
        ]
        results = pl.pallas_call(
            functools.partial(kernel, sections, replicas, heads),
            out_shape=(
                jax.ShapeDtypeStruct(stream.shape, BF16),
                jax.ShapeDtypeStruct(stream.shape, BF16),
                jax.ShapeDtypeStruct((1, grad_rows, kv_width), F32),
            ),
            in_specs=[pl.BlockSpec(memory_space=pl.ANY)] * 12,
            out_specs=(pl.BlockSpec(memory_space=pl.ANY),) * 3,
            scratch_shapes=scratch,
            compiler_params=pltpu.CompilerParams(
                collective_id=0, has_side_effects=True, vmem_limit_bytes=56 * 1024 * 1024
            ),
        )(
            segments,
            stream,
            entering,
            pending,
            gain,
            wq,
            wk,
            wv,
            wo,
            scale,
            blend,
            cotangent,
        )
        return pl.pallas_call(
            store_kernel,
            out_shape=tuple(jax.ShapeDtypeStruct(r.shape, r.dtype) for r in results),
            in_specs=[pl.BlockSpec(memory_space=pl.ANY)] * 3,
            out_specs=(pl.BlockSpec(memory_space=pl.ANY),) * 3,
            scratch_shapes=[pltpu.VMEM(r.shape[1:], r.dtype) for r in results]
            + [dma((3 * STORE_BLOCKS,)), dma((3 * STORE_BLOCKS,))],
            compiler_params=pltpu.CompilerParams(vmem_limit_bytes=56 * 1024 * 1024),
        )(*results)

    return jax.shard_map(
        per_device,
        mesh=mesh,
        in_specs=(
            P(None, "dp"),
            P("section", "dp", "head"),
            P("dp", None),
            P("section", "dp", "head"),
            P("section", None),
            P("section", None, "head"),
            P("section", None, "head"),
            P("section", None, "head"),
            P("section", None, "head"),
            P("section", "head"),
            P("section", "head"),
            P("section", None, "dp", "head"),
        ),
        out_specs=(
            P("section", "dp", "head"),
            P("section", "dp", "head"),
            P("section", "dp", "head"),
        ),
        check_vma=False,
    )
```

```python
import functools
import math

import jax
import jax.numpy as jnp
from jax import lax
from jax.experimental import pallas as pl
from jax.experimental.pallas import tpu as pltpu
from jax.sharding import PartitionSpec as P

HEAD_WIDTH = 128
CHUNK = 256
STORE_BLOCKS = 2
EPSILON = 1e-06
F32 = jnp.float32
BF16 = jnp.bfloat16


def dot(a, b):
    return jnp.dot(a, b, preferred_element_type=F32)


def split_high_low(values):
    high = values.astype(BF16)
    return high, (values - high.astype(F32)).astype(BF16)


def kernel(
    sections,
    replicas,
    heads,
    seg_hbm,
    x_hbm,
    entering_hbm,
    pending_hbm,
    gain_hbm,
    wq_hbm,
    wk_hbm,
    wv_hbm,
    wo_hbm,
    scale_hbm,
    blend_hbm,
    cot_hbm,
    out1_hbm,
    out2_hbm,
    grad_hbm,
    seg,
    gain,
    scale,
    blend,
    wq,
    wk,
    wv,
    wo,
    x1,
    x2,
    f1,
    f2,
    normed1,
    normed2,
    acc,
    att1,
    att2,
    out1,
    out2,
    proj,
    rows_n,
    rows_c,
    grad,
    local_sem,
    weight_sem,
    enter_sem,
    out_sem,
    x_send,
    x_recv,
    c_send,
    c_recv,
    n_send,
    n_recv,
    a_send,
    a_recv,
    z_send,
    z_recv,
    f_send,
    f_recv,
    v_send,
    v_recv,
    h_send,
    h_recv,
):
    section = lax.axis_index("section")
    replica = lax.axis_index("dp")
    me = lax.axis_index("head")
    tokens, width = x1.shape[1], x1.shape[2]
    model = width * heads
    q_width, kv_width = wq.shape[1], wk.shape[1]
    kv_heads = kv_width // HEAD_WIDTH
    group = q_width // kv_width
    grad_rows = model // replicas
    chunks = width // CHUNK
    is_first = section == 0
    not_first = section > 0
    not_last = section < sections - 1

    def local(src, dst, sem):
        copy = pltpu.make_async_copy(src, dst, sem)
        copy.start()
        return copy

    def remote(src, dst, send, recv, where):
        return pltpu.make_async_remote_copy(
            src_ref=src,
            dst_ref=dst,
            send_sem=send,
            recv_sem=recv,
            device_id=where,
            device_id_type=pl.DeviceIdType.MESH,
        )

    def head_at(step):
        return lax.rem(me + step, heads)

    def replica_at(step):
        return lax.rem(replica + step, replicas)

    x_load = local(x_hbm.at[0], x1.at[me], local_sem.at[0])
    gain_load = local(gain_hbm, gain, local_sem.at[1])
    weight_loads = []
    for step in range(heads):
        first = pl.multiple_of(lax.rem(me + heads - step, heads) * width, CHUNK)
        half = width // 2
        blocks = [(wk_hbm, wk, first, width), (wv_hbm, wv, first, width)]
        blocks += [(wq_hbm, wq, first + i * half, half) for i in range(2)]
        weight_loads.append(
            [
                local(
                    source.at[0, pl.ds(pl.multiple_of(row, CHUNK), size)],
                    target.at[pl.ds(pl.multiple_of(row, CHUNK), size)],
                    weight_sem.at[4 * step + i],
                )
                for i, (source, target, row, size) in enumerate(blocks)
            ]
        )
    seg_load = local(seg_hbm, seg, local_sem.at[2])
    scale_load = local(scale_hbm, scale, local_sem.at[3])
    blend_load = local(blend_hbm, blend, local_sem.at[4])
    cot_load = local(cot_hbm.at[0], rows_c.at[replica], local_sem.at[5])
    f1_load = pltpu.make_async_copy(pending_hbm.at[0], f1, local_sem.at[6])

    @pl.when(not_first)
    def _():
        f1_load.start()

    quarter = model // 4
    wo_loads = [
        local(
            wo_hbm.at[0, pl.ds(i * quarter, quarter)],
            wo.at[pl.ds(i * quarter, quarter)],
            weight_sem.at[4 * heads + i],
        )
        for i in range(4)
    ]
    enter_loads = [
        pltpu.make_async_copy(
            entering_hbm.at[:, pl.ds(h * width, width)], x2.at[h], enter_sem.at[h]
        )
        for h in range(heads)
    ]

    @pl.when(is_first)
    def _():
        for load in enter_loads:
            load.start()
        f2[...] = jnp.zeros_like(f2)

    barrier = pltpu.get_barrier_semaphore()

    def greet(where):
        pl.semaphore_signal(barrier, inc=1, device_id=where, device_id_type=pl.DeviceIdType.MESH)

    for step in range(1, heads):
        greet((section, replica, head_at(step)))
    for step in range(1, replicas):
        greet((section, replica_at(step), me))

    @pl.when(not_first)
    def _():
        greet((section - 1, replica, me))

    @pl.when(not_last)
    def _():
        greet((section + 1, replica, me))

    pl.semaphore_wait(
        barrier,
        heads - 1 + replicas - 1 + not_first.astype(jnp.int32) + not_last.astype(jnp.int32),
    )

    x_copies = []
    for step in range(1, heads):
        copy = remote(
            x_hbm.at[0],
            x1.at[me],
            x_send.at[step - 1],
            x_recv.at[step - 1],
            (section, replica, head_at(step)),
        )
        copy.start()
        x_copies.append(copy)
    value_copy = remote(f1, f2, v_send.at[0], v_recv.at[0], (section + 1, replica, me))

    def send_cotangents(turn):
        copies = []
        for step in range(1, replicas):
            copy = remote(
                cot_hbm.at[0, turn],
                rows_c.at[replica, turn],
                c_send.at[turn, step - 1],
                c_recv.at[turn, step - 1],
                (section, replica_at(step), me),
            )
            copy.start()
            copies.append(copy)
        return copies

    c1_copies = send_cotangents(0)

    k_at, v_at = q_width, q_width + kv_width
    weights_at = ((wk, k_at, kv_width), (wv, v_at, kv_width), (wq, 0, q_width))

    def project(pieces, size, is_start):
        scaled = []
        for part, first_row in pieces:
            rows = pl.ds(pl.multiple_of(first_row, CHUNK), size)
            scaled.append(((part * gain[:, rows]).astype(BF16), rows))
        for weight, at, columns in weights_at:
            product = dot(scaled[0][0], weight[scaled[0][1], :])
            for piece, rows in scaled[1:]:
                product += dot(piece, weight[rows, :])
            if is_start:
                acc[:, pl.ds(at, columns)] = product
            else:
                acc[:, pl.ds(at, columns)] += product

    def normalize(stream, squares, normed):
        inverse = lax.rsqrt(squares / model + EPSILON)
        for h in range(heads):
            columns = pl.ds(h * width, width)
            normed[:, columns] = (stream[h].astype(F32) * inverse * gain[:, columns]).astype(BF16)
        return inverse

    share_rows = tokens // heads
    share = pl.ds(pl.multiple_of(me * share_rows, share_rows), share_rows)

    def hand_on(copies, turn):
        handed = []
        for step in range(1, replicas):
            copies[step - 1].wait_recv()
            block = rows_n.at[turn, lax.rem(replica + replicas - step, replicas), share]
            for hop in range(1, heads):
                copy = remote(
                    block,
                    block,
                    h_send.at[turn, step - 1, hop - 1],
                    h_recv.at[turn, step - 1, hop - 1],
                    (section, replica, head_at(hop)),
                )
                copy.start()
                handed.append(copy)
        return handed

    def send_normed(normed, turn):
        copies = []
        for step in range(1, replicas):
            peer = replica_at(step)
            first = pl.multiple_of(peer * grad_rows, 128)
            copy = remote(
                normed.at[share, pl.ds(first, grad_rows)],
                rows_n.at[turn, replica, share],
                n_send.at[turn, step - 1],
                n_recv.at[turn, step - 1],
                (section, peer, me),
            )
            copy.start()
            copies.append(copy)
        first = pl.multiple_of(replica * grad_rows, 128)
        rows_n[turn, replica] = normed[:, pl.ds(first, grad_rows)]
        return copies

    gain_load.wait()
    x_load.wait()
    for load in weight_loads[0]:
        load.wait()
    part = x1[me].astype(F32)
    squares = jnp.sum(part * part, axis=-1, keepdims=True)
    project([(part, me * width)], width, True)
    for copy in x_copies:
        copy.wait_recv()
    for step in range(1, heads):
        part = x1[lax.rem(me + heads - step, heads)].astype(F32)
        squares += jnp.sum(part * part, axis=-1, keepdims=True)
    inverse1 = normalize(x1, squares, normed1)
    n1_copies = send_normed(normed1, 0)
    c2_copies = send_cotangents(1)
    for step in range(1, heads):
        for load in weight_loads[step]:
            load.wait()
        owner = lax.rem(me + heads - step, heads)
        project([(x1[owner].astype(F32), owner * width)], width, False)

    seg_load.wait()
    scale_load.wait()
    blend_load.wait()

    @pl.when(not_first)
    def _():
        f1_load.wait()

    @pl.when(is_first)
    def _():
        f1[...] = (acc[:, pl.ds(v_at, kv_width)] * inverse1).astype(BF16)

    @pl.when(not_last)
    def _():
        value_copy.start()

    causal = lax.broadcasted_iota(jnp.int32, (tokens, tokens), 0) >= lax.broadcasted_iota(
        jnp.int32, (tokens, tokens), 1
    )

    ones = jnp.ones((2 * HEAD_WIDTH, HEAD_WIDTH), BF16)
    mixed_ones = jnp.ones((tokens, HEAD_WIDTH), BF16)

    def unit_rows(values):
        total = dot(jnp.concatenate(split_high_low(values * values), axis=1), ones)
        return values * lax.rsqrt(total / HEAD_WIDTH + EPSILON)

    def attend(segment_index, earlier, att, turn, inverse):
        row = seg[pl.ds(segment_index, 1), :].astype(F32)
        across = jnp.broadcast_to(row, (tokens, tokens))
        allowed = causal & (across == across.T)
        queries, keys, mixes = [], [], []
        for g in range(kv_heads):
            kv_columns = pl.ds(g * HEAD_WIDTH, HEAD_WIDTH)
            values = acc[:, pl.ds(v_at + g * HEAD_WIDTH, HEAD_WIDTH)] * inverse
            blended = values + blend[:, g : g + 1] * earlier[:, kv_columns].astype(F32)
            mixed_values = jnp.where(is_first, values, blended).astype(BF16)
            mixes.append(jnp.concatenate([mixed_values, mixed_ones], axis=1))
            stacked = [acc[:, pl.ds(k_at + g * HEAD_WIDTH, HEAD_WIDTH)] * inverse]
            for h in range(g * group, (g + 1) * group):
                stacked.append(acc[:, pl.ds(h * HEAD_WIDTH, HEAD_WIDTH)] * inverse)
            unit = unit_rows(jnp.concatenate(stacked, axis=0))
            key_high, key_low = split_high_low(unit[:tokens])
            keys.append(jnp.concatenate([key_high, key_high, key_low], axis=1))
            parts = []
            for j in range(group):
                h = g * group + j
                query_high, query_low = split_high_low(
                    unit[(j + 1) * tokens : (j + 2) * tokens]
                    * (scale[:, h : h + 1] / math.sqrt(HEAD_WIDTH))
                )
                parts.append(jnp.concatenate([query_high, query_low, query_high], axis=1))
            queries.append(jnp.concatenate(parts, axis=0))
        scores = [
            lax.dot_general(q, k, (((1,), (1,)), ((), ())), preferred_element_type=F32)
            for q, k in zip(queries, keys)
        ]
        exponents = []
        for score in scores:
            score = jnp.where(allowed[None], score.reshape(group, tokens, tokens), -1e30)
            top = jnp.max(score, axis=-1, keepdims=True)
            exponents.append(jnp.exp(score - top).astype(BF16).reshape(group * tokens, tokens))
        results = [dot(e, m) for e, m in zip(exponents, mixes)]
        for g, result in enumerate(results):
            result = (result[:, :HEAD_WIDTH] / result[:, HEAD_WIDTH:]).astype(BF16)
            for j in range(group):
                att[me, :, pl.ds((g * group + j) * HEAD_WIDTH, HEAD_WIDTH)] = result[
                    j * tokens : (j + 1) * tokens
                ]
        for step in range(1, heads):
            copy = remote(
                att.at[me],
                att.at[me],
                a_send.at[turn, step - 1],
                a_recv.at[turn, step - 1],
                (section, replica, head_at(step)),
            )
            copy.start()
            a_copies.append((turn, copy))

    a_copies = []
    attend(section, f1, att1, 0, inverse1)

    def own_tile(att, c):
        rows = pl.ds(pl.multiple_of(me * q_width, q_width), q_width)
        columns = pl.ds(c * CHUNK, CHUNK)
        proj[:, columns] = dot(att[me], wo[rows, columns])

    def whole_tile(att, stream, c):
        columns = pl.ds(c * CHUNK, CHUNK)
        total = proj[:, columns] + stream[me, :, columns].astype(F32)
        for step in range(1, heads):
            peer = lax.rem(me + heads - step, heads)
            rows = pl.ds(pl.multiple_of(peer * q_width, q_width), q_width)
            total += dot(att[peer], wo[rows, columns])
        return total.astype(BF16)

    def z_copy(c):
        columns = pl.ds(c * CHUNK, CHUNK)
        return remote(
            out1.at[:, columns],
            x2.at[me, :, columns],
            z_send.at[c],
            z_recv.at[c],
            (section + 1, replica, me),
        )

    for load in wo_loads:
        load.wait()
    ahead = chunks // 2
    for c in range(ahead):
        own_tile(att1, c)
    for turn, copy in a_copies:
        if turn == 0:
            copy.wait_recv()
    for c in range(chunks):
        if c >= ahead:
            own_tile(att1, c)
        out1[:, pl.ds(c * CHUNK, CHUNK)] = whole_tile(att1, x1, c)

        @pl.when(not_last)
        def _(c=c):
            z_copy(c).start()

    out1_store = local(out1, out1_hbm.at[0], out_sem.at[0])

    def grad_part(turn):
        features = jnp.concatenate([rows_n[turn, p] for p in range(replicas)], axis=0)
        cotangents = jnp.concatenate([rows_c[p, turn] for p in range(replicas)], axis=0)
        return lax.dot_general(
            features, cotangents, (((0,), (0,)), ((), ())), preferred_element_type=F32
        )

    cot_load.wait()

    def forward(step, c):
        columns = pl.ds(c * CHUNK, CHUNK)
        return remote(
            x2.at[me, :, columns],
            x2.at[me, :, columns],
            f_send.at[step - 1, c],
            f_recv.at[step - 1, c],
            (section, replica, head_at(step)),
        )

    @pl.when(is_first)
    def _():
        for load in enter_loads:
            load.wait()

    squares = jnp.zeros((tokens, 1), F32)
    for c in range(chunks + 1):
        @pl.when(not_first)
        def _(c=c):
            if c < chunks:
                z_copy(c).wait_recv()
                for step in range(1, heads):
                    forward(step, c).start()
            if c > 0:
                for step in range(1, heads):
                    forward(step, c - 1).wait_recv()

        pieces = []
        for step in range(heads):
            at = c if step == 0 else c - 1
            if 0 <= at < chunks:
                owner = lax.rem(me + heads - step, heads)
                part = x2[owner, :, pl.ds(at * CHUNK, CHUNK)].astype(F32)
                squares += jnp.sum(part * part, axis=-1, keepdims=True)
                pieces.append((part, owner * width + at * CHUNK))
        if c == chunks:
            inverse2 = normalize(x2, squares, normed2)
            n2_copies = send_normed(normed2, 1)
        project(pieces, CHUNK, c == 0)
        if c == chunks - 2:
            handed1 = hand_on(n1_copies, 0)
        if c == chunks - 1:
            for copy in c1_copies + handed1:
                copy.wait_recv()
            grad[...] = grad_part(0)

    @pl.when(not_first)
    def _():
        value_copy.wait_recv()

    attend(lax.rem(section + sections, sections + 1), f2, att2, 1, inverse2)
    for c in range(chunks):
        own_tile(att2, c)
    for turn, copy in a_copies:
        if turn == 1:
            copy.wait_recv()
    for c in range(chunks):
        if c == chunks // 2:
            handed2 = hand_on(n2_copies, 1)
        out2[:, pl.ds(c * CHUNK, CHUNK)] = whole_tile(att2, x2, c)
    out2_store = local(out2, out2_hbm.at[0], out_sem.at[1])

    for copy in c2_copies + handed2:
        copy.wait_recv()
    grad[...] += grad_part(1)
    grad_store = local(grad, grad_hbm.at[0], out_sem.at[2])

    for copy in x_copies + c1_copies + c2_copies + n1_copies + n2_copies + handed1 + handed2:
        copy.wait_send()
    for _, copy in a_copies:
        copy.wait_send()

    @pl.when(not_last)
    def _():
        value_copy.wait_send()
        for c in range(chunks):
            z_copy(c).wait_send()

    @pl.when(not_first)
    def _():
        for c in range(chunks):
            for step in range(1, heads):
                forward(step, c).wait_send()

    out1_store.wait()
    out2_store.wait()
    grad_store.wait()


def store_kernel(*refs):
    sources, targets, buffers, load_sem, store_sem = refs[:3], refs[3:6], refs[6:9], refs[9], refs[10]
    loads, stores = [], []
    for source, target, buffer in zip(sources, targets, buffers):
        rows = source.shape[1] // STORE_BLOCKS
        for i in range(STORE_BLOCKS):
            block, n = pl.ds(i * rows, rows), len(loads)
            loads.append(
                pltpu.make_async_copy(source.at[0, block], buffer.at[block], load_sem.at[n])
            )
            stores.append(
                pltpu.make_async_copy(buffer.at[block], target.at[0, block], store_sem.at[n])
            )
    for load in loads:
        load.start()
    for load, store in zip(loads, stores):
        load.wait()
        store.start()
    for store in stores:
        store.wait()


def solution(mesh):
    sections, replicas, heads = (mesh.shape[a] for a in ("section", "dp", "head"))

    def per_device(
        segments,
        stream,
        entering,
        pending,
        gain,
        wq,
        wk,
        wv,
        wo,
        scale,
        blend,
        cotangent,
    ):
        _, tokens, width = stream.shape
        model = width * heads
        q_width, kv_width = wq.shape[2], wk.shape[2]
        grad_rows = model // replicas
        chunks = width // CHUNK
        others = heads - 1
        peers = replicas - 1
        dma = pltpu.SemaphoreType.DMA
        scratch = [
            pltpu.VMEM(segments.shape, jnp.int32),
            pltpu.VMEM(gain.shape, F32),
            pltpu.VMEM(scale.shape, F32),
            pltpu.VMEM(blend.shape, F32),
            pltpu.VMEM((model, q_width), BF16),
            pltpu.VMEM((model, kv_width), BF16),
            pltpu.VMEM((model, kv_width), BF16),
            pltpu.VMEM((model, width), BF16),
            pltpu.VMEM((heads, tokens, width), BF16),
            pltpu.VMEM((heads, tokens, width), BF16),
            pltpu.VMEM((tokens, kv_width), BF16),
            pltpu.VMEM((tokens, kv_width), BF16),
            pltpu.VMEM((tokens, model), BF16),
            pltpu.VMEM((tokens, model), BF16),
            pltpu.VMEM((tokens, q_width + 2 * kv_width), F32),
            pltpu.VMEM((heads, tokens, q_width), BF16),
            pltpu.VMEM((heads, tokens, q_width), BF16),
            pltpu.VMEM((tokens, width), BF16),
            pltpu.VMEM((tokens, width), BF16),
            pltpu.VMEM((tokens, width), F32),
            pltpu.VMEM((2, replicas, tokens, grad_rows), BF16),
            pltpu.VMEM((replicas, 2, tokens, kv_width), BF16),
            pltpu.VMEM((grad_rows, kv_width), F32),
            dma((7,)),
            dma((4 * heads + 4,)),
            dma((heads,)),
            dma((3,)),
            dma((others,)),
            dma((others,)),
            dma((2, peers)),
            dma((2, peers)),
            dma((2, peers)),
            dma((2, peers)),
            dma((2, others)),
            dma((2, others)),
            dma((chunks,)),
            dma((chunks,)),
            dma((others, chunks)),
            dma((others, chunks)),
            dma((1,)),
            dma((1,)),
            dma((2, peers, others)),
            dma((2, peers, others)),
        ]
        results = pl.pallas_call(
            functools.partial(kernel, sections, replicas, heads),
            out_shape=(
                jax.ShapeDtypeStruct(stream.shape, BF16),
                jax.ShapeDtypeStruct(stream.shape, BF16),
                jax.ShapeDtypeStruct((1, grad_rows, kv_width), F32),
            ),
            in_specs=[pl.BlockSpec(memory_space=pl.ANY)] * 12,
            out_specs=(pl.BlockSpec(memory_space=pl.ANY),) * 3,
            scratch_shapes=scratch,
            compiler_params=pltpu.CompilerParams(
                collective_id=0, has_side_effects=True, vmem_limit_bytes=56 * 1024 * 1024
            ),
        )(
            segments,
            stream,
            entering,
            pending,
            gain,
            wq,
            wk,
            wv,
            wo,
            scale,
            blend,
            cotangent,
        )
        return pl.pallas_call(
            store_kernel,
            out_shape=tuple(jax.ShapeDtypeStruct(r.shape, r.dtype) for r in results),
            in_specs=[pl.BlockSpec(memory_space=pl.ANY)] * 3,
            out_specs=(pl.BlockSpec(memory_space=pl.ANY),) * 3,
            scratch_shapes=[pltpu.VMEM(r.shape[1:], r.dtype) for r in results]
            + [dma((3 * STORE_BLOCKS,)), dma((3 * STORE_BLOCKS,))],
            compiler_params=pltpu.CompilerParams(vmem_limit_bytes=56 * 1024 * 1024),
        )(*results)

    return jax.shard_map(
        per_device,
        mesh=mesh,
        in_specs=(
            P(None, "dp"),
            P("section", "dp", "head"),
            P("dp", None),
            P("section", "dp", "head"),
            P("section", None),
            P("section", None, "head"),
            P("section", None, "head"),
            P("section", None, "head"),
            P("section", None, "head"),
            P("section", "head"),
            P("section", "head"),
            P("section", None, "dp", "head"),
        ),
        out_specs=(
            P("section", "dp", "head"),
            P("section", "dp", "head"),
            P("section", "dp", "head"),
        ),
        check_vma=False,
    )
```

```python
import functools
import math

import jax
import jax.numpy as jnp
from jax import lax
from jax.experimental import pallas as pl
from jax.experimental.pallas import tpu as pltpu
from jax.sharding import PartitionSpec as P

HEAD_WIDTH = 128
CHUNK = 256
STORE_BLOCKS = 2
EPSILON = 1e-06
F32 = jnp.float32
BF16 = jnp.bfloat16


def dot(a, b):
    return jnp.dot(a, b, preferred_element_type=F32)


def split_high_low(values):
    high = values.astype(BF16)
    return high, (values - high.astype(F32)).astype(BF16)


def kernel(
    sections,
    replicas,
    heads,
    seg_hbm,
    x_hbm,
    entering_hbm,
    pending_hbm,
    gain_hbm,
    wq_hbm,
    wk_hbm,
    wv_hbm,
    wo_hbm,
    scale_hbm,
    blend_hbm,
    cot_hbm,
    out1_hbm,
    out2_hbm,
    grad_hbm,
    seg,
    gain,
    scale,
    blend,
    wq,
    wk,
    wv,
    wo,
    x1,
    x2,
    f1,
    f2,
    normed1,
    normed2,
    acc,
    att1,
    att2,
    out1,
    out2,
    proj,
    rows_n,
    rows_c,
    grad,
    local_sem,
    weight_sem,
    enter_sem,
    out_sem,
    x_send,
    x_recv,
    c_send,
    c_recv,
    n_send,
    n_recv,
    a_send,
    a_recv,
    z_send,
    z_recv,
    f_send,
    f_recv,
    v_send,
    v_recv,
    h_send,
    h_recv,
):
    section = lax.axis_index("section")
    replica = lax.axis_index("dp")
    me = lax.axis_index("head")
    tokens, width = x1.shape[1], x1.shape[2]
    model = width * heads
    q_width, kv_width = wq.shape[1], wk.shape[1]
    kv_heads = kv_width // HEAD_WIDTH
    group = q_width // kv_width
    grad_rows = model // replicas
    chunks = width // CHUNK
    is_first = section == 0
    not_first = section > 0
    not_last = section < sections - 1

    def local(src, dst, sem):
        copy = pltpu.make_async_copy(src, dst, sem)
        copy.start()
        return copy

    def remote(src, dst, send, recv, where):
        return pltpu.make_async_remote_copy(
            src_ref=src,
            dst_ref=dst,
            send_sem=send,
            recv_sem=recv,
            device_id=where,
            device_id_type=pl.DeviceIdType.MESH,
        )

    def head_at(step):
        return lax.rem(me + step, heads)

    def replica_at(step):
        return lax.rem(replica + step, replicas)

    x_load = local(x_hbm.at[0], x1.at[me], local_sem.at[0])
    gain_load = local(gain_hbm, gain, local_sem.at[1])
    weight_loads = []
    for step in range(heads):
        first = pl.multiple_of(lax.rem(me + heads - step, heads) * width, CHUNK)
        half = width // 2
        blocks = [(wk_hbm, wk, first, width), (wv_hbm, wv, first, width)]
        blocks += [(wq_hbm, wq, first + i * half, half) for i in range(2)]
        weight_loads.append(
            [
                local(
                    source.at[0, pl.ds(pl.multiple_of(row, CHUNK), size)],
                    target.at[pl.ds(pl.multiple_of(row, CHUNK), size)],
                    weight_sem.at[4 * step + i],
                )
                for i, (source, target, row, size) in enumerate(blocks)
            ]
        )
    seg_load = local(seg_hbm, seg, local_sem.at[2])
    scale_load = local(scale_hbm, scale, local_sem.at[3])
    blend_load = local(blend_hbm, blend, local_sem.at[4])
    cot_load = local(cot_hbm.at[0], rows_c.at[replica], local_sem.at[5])
    f1_load = pltpu.make_async_copy(pending_hbm.at[0], f1, local_sem.at[6])

    @pl.when(not_first)
    def _():
        f1_load.start()

    quarter = model // 4
    wo_loads = [
        local(
            wo_hbm.at[0, pl.ds(i * quarter, quarter)],
            wo.at[pl.ds(i * quarter, quarter)],
            weight_sem.at[4 * heads + i],
        )
        for i in range(4)
    ]
    enter_loads = [
        pltpu.make_async_copy(
            entering_hbm.at[:, pl.ds(h * width, width)], x2.at[h], enter_sem.at[h]
        )
        for h in range(heads)
    ]

    @pl.when(is_first)
    def _():
        for load in enter_loads:
            load.start()
        f2[...] = jnp.zeros_like(f2)

    barrier = pltpu.get_barrier_semaphore()

    def greet(where):
        pl.semaphore_signal(barrier, inc=1, device_id=where, device_id_type=pl.DeviceIdType.MESH)

    for step in range(1, heads):
        greet((section, replica, head_at(step)))
    for step in range(1, replicas):
        greet((section, replica_at(step), me))

    @pl.when(not_first)
    def _():
        greet((section - 1, replica, me))

    @pl.when(not_last)
    def _():
        greet((section + 1, replica, me))

    pl.semaphore_wait(
        barrier,
        heads - 1 + replicas - 1 + not_first.astype(jnp.int32) + not_last.astype(jnp.int32),
    )

    x_copies = []
    for step in range(1, heads):
        copy = remote(
            x_hbm.at[0],
            x1.at[me],
            x_send.at[step - 1],
            x_recv.at[step - 1],
            (section, replica, head_at(step)),
        )
        copy.start()
        x_copies.append(copy)
    value_copy = remote(f1, f2, v_send.at[0], v_recv.at[0], (section + 1, replica, me))

    def send_cotangents(turn):
        copies = []
        for step in range(1, replicas):
            copy = remote(
                cot_hbm.at[0, turn],
                rows_c.at[replica, turn],
                c_send.at[turn, step - 1],
                c_recv.at[turn, step - 1],
                (section, replica_at(step), me),
            )
            copy.start()
            copies.append(copy)
        return copies

    c1_copies = send_cotangents(0)

    k_at, v_at = q_width, q_width + kv_width
    weights_at = ((wk, k_at, kv_width), (wv, v_at, kv_width), (wq, 0, q_width))

    def project(pieces, size, is_start):
        scaled = []
        for part, first_row in pieces:
            rows = pl.ds(pl.multiple_of(first_row, CHUNK), size)
            scaled.append(((part * gain[:, rows]).astype(BF16), rows))
        for weight, at, columns in weights_at:
            product = dot(scaled[0][0], weight[scaled[0][1], :])
            for piece, rows in scaled[1:]:
                product += dot(piece, weight[rows, :])
            if is_start:
                acc[:, pl.ds(at, columns)] = product
            else:
                acc[:, pl.ds(at, columns)] += product

    def normalize(stream, squares, normed):
        inverse = lax.rsqrt(squares / model + EPSILON)
        for h in range(heads):
            columns = pl.ds(h * width, width)
            normed[:, columns] = (stream[h].astype(F32) * inverse * gain[:, columns]).astype(BF16)
        return inverse

    share_rows = tokens // heads
    share = pl.ds(pl.multiple_of(me * share_rows, share_rows), share_rows)

    def hand_on(copies, turn):
        handed = []
        for step in range(1, replicas):
            copies[step - 1].wait_recv()
            block = rows_n.at[turn, lax.rem(replica + replicas - step, replicas), share]
            for hop in range(1, heads):
                copy = remote(
                    block,
                    block,
                    h_send.at[turn, step - 1, hop - 1],
                    h_recv.at[turn, step - 1, hop - 1],
                    (section, replica, head_at(hop)),
                )
                copy.start()
                handed.append(copy)
        return handed

    def send_normed(normed, turn):
        copies = []
        for step in range(1, replicas):
            peer = replica_at(step)
            first = pl.multiple_of(peer * grad_rows, 128)
            copy = remote(
                normed.at[share, pl.ds(first, grad_rows)],
                rows_n.at[turn, replica, share],
                n_send.at[turn, step - 1],
                n_recv.at[turn, step - 1],
                (section, peer, me),
            )
            copy.start()
            copies.append(copy)
        first = pl.multiple_of(replica * grad_rows, 128)
        rows_n[turn, replica] = normed[:, pl.ds(first, grad_rows)]
        return copies

    gain_load.wait()
    x_load.wait()
    for load in weight_loads[0]:
        load.wait()
    part = x1[me].astype(F32)
    squares = jnp.sum(part * part, axis=-1, keepdims=True)
    project([(part, me * width)], width, True)
    for copy in x_copies:
        copy.wait_recv()
    for step in range(1, heads):
        part = x1[lax.rem(me + heads - step, heads)].astype(F32)
        squares += jnp.sum(part * part, axis=-1, keepdims=True)
    inverse1 = normalize(x1, squares, normed1)
    n1_copies = send_normed(normed1, 0)
    c2_copies = send_cotangents(1)
    for step in range(1, heads):
        for load in weight_loads[step]:
            load.wait()
        owner = lax.rem(me + heads - step, heads)
        project([(x1[owner].astype(F32), owner * width)], width, False)

    seg_load.wait()
    scale_load.wait()
    blend_load.wait()

    @pl.when(not_first)
    def _():
        f1_load.wait()

    @pl.when(is_first)
    def _():
        f1[...] = (acc[:, pl.ds(v_at, kv_width)] * inverse1).astype(BF16)

    @pl.when(not_last)
    def _():
        value_copy.start()

    causal = lax.broadcasted_iota(jnp.int32, (tokens, tokens), 0) >= lax.broadcasted_iota(
        jnp.int32, (tokens, tokens), 1
    )

    ones = jnp.ones((2 * HEAD_WIDTH, HEAD_WIDTH), BF16)
    mixed_ones = jnp.ones((tokens, HEAD_WIDTH), BF16)

    def unit_rows(values):
        total = dot(jnp.concatenate(split_high_low(values * values), axis=1), ones)
        return values * lax.rsqrt(total / HEAD_WIDTH + EPSILON)

    def attend(segment_index, earlier, att, turn, inverse):
        row = seg[pl.ds(segment_index, 1), :].astype(F32)
        across = jnp.broadcast_to(row, (tokens, tokens))
        allowed = causal & (across == across.T)
        queries, keys, mixes = [], [], []
        for g in range(kv_heads):
            kv_columns = pl.ds(g * HEAD_WIDTH, HEAD_WIDTH)
            values = acc[:, pl.ds(v_at + g * HEAD_WIDTH, HEAD_WIDTH)] * inverse
            blended = values + blend[:, g : g + 1] * earlier[:, kv_columns].astype(F32)
            mixed_values = jnp.where(is_first, values, blended).astype(BF16)
            mixes.append(jnp.concatenate([mixed_values, mixed_ones], axis=1))
            stacked = [acc[:, pl.ds(k_at + g * HEAD_WIDTH, HEAD_WIDTH)] * inverse]
            for h in range(g * group, (g + 1) * group):
                stacked.append(acc[:, pl.ds(h * HEAD_WIDTH, HEAD_WIDTH)] * inverse)
            unit = unit_rows(jnp.concatenate(stacked, axis=0))
            key_high, key_low = split_high_low(unit[:tokens])
            keys.append(jnp.concatenate([key_high, key_high, key_low], axis=1))
            parts = []
            for j in range(group):
                h = g * group + j
                query_high, query_low = split_high_low(
                    unit[(j + 1) * tokens : (j + 2) * tokens]
                    * (scale[:, h : h + 1] / math.sqrt(HEAD_WIDTH))
                )
                parts.append(jnp.concatenate([query_high, query_low, query_high], axis=1))
            queries.append(jnp.concatenate(parts, axis=0))
        scores = [
            lax.dot_general(q, k, (((1,), (1,)), ((), ())), preferred_element_type=F32)
            for q, k in zip(queries, keys)
        ]
        exponents = []
        for score in scores:
            score = jnp.where(allowed[None], score.reshape(group, tokens, tokens), -1e30)
            top = jnp.max(score, axis=-1, keepdims=True)
            exponents.append(jnp.exp(score - top).astype(BF16).reshape(group * tokens, tokens))
        results = [dot(e, m) for e, m in zip(exponents, mixes)]
        for g, result in enumerate(results):
            result = (result[:, :HEAD_WIDTH] / result[:, HEAD_WIDTH:]).astype(BF16)
            for j in range(group):
                att[me, :, pl.ds((g * group + j) * HEAD_WIDTH, HEAD_WIDTH)] = result[
                    j * tokens : (j + 1) * tokens
                ]
        for step in range(1, heads):
            copy = remote(
                att.at[me],
                att.at[me],
                a_send.at[turn, step - 1],
                a_recv.at[turn, step - 1],
                (section, replica, head_at(step)),
            )
            copy.start()
            a_copies.append((turn, copy))

    a_copies = []
    attend(section, f1, att1, 0, inverse1)

    def own_tile(att, c):
        rows = pl.ds(pl.multiple_of(me * q_width, q_width), q_width)
        columns = pl.ds(c * CHUNK, CHUNK)
        proj[:, columns] = dot(att[me], wo[rows, columns])

    def whole_tile(att, stream, c):
        columns = pl.ds(c * CHUNK, CHUNK)
        total = proj[:, columns] + stream[me, :, columns].astype(F32)
        for step in range(1, heads):
            peer = lax.rem(me + heads - step, heads)
            rows = pl.ds(pl.multiple_of(peer * q_width, q_width), q_width)
            total += dot(att[peer], wo[rows, columns])
        return total.astype(BF16)

    def z_copy(c):
        columns = pl.ds(c * CHUNK, CHUNK)
        return remote(
            out1.at[:, columns],
            x2.at[me, :, columns],
            z_send.at[c],
            z_recv.at[c],
            (section + 1, replica, me),
        )

    for load in wo_loads:
        load.wait()
    ahead = 1
    for c in range(ahead):
        own_tile(att1, c)
    for turn, copy in a_copies:
        if turn == 0:
            copy.wait_recv()
    for c in range(chunks):
        if c >= ahead:
            own_tile(att1, c)
        out1[:, pl.ds(c * CHUNK, CHUNK)] = whole_tile(att1, x1, c)

        @pl.when(not_last)
        def _(c=c):
            z_copy(c).start()

    out1_store = local(out1, out1_hbm.at[0], out_sem.at[0])

    def grad_part(turn):
        features = jnp.concatenate([rows_n[turn, p] for p in range(replicas)], axis=0)
        cotangents = jnp.concatenate([rows_c[p, turn] for p in range(replicas)], axis=0)
        return lax.dot_general(
            features, cotangents, (((0,), (0,)), ((), ())), preferred_element_type=F32
        )

    cot_load.wait()

    def forward(step, c):
        columns = pl.ds(c * CHUNK, CHUNK)
        return remote(
            x2.at[me, :, columns],
            x2.at[me, :, columns],
            f_send.at[step - 1, c],
            f_recv.at[step - 1, c],
            (section, replica, head_at(step)),
        )

    @pl.when(is_first)
    def _():
        for load in enter_loads:
            load.wait()

    squares = jnp.zeros((tokens, 1), F32)
    for c in range(chunks + 1):
        @pl.when(not_first)
        def _(c=c):
            if c < chunks:
                z_copy(c).wait_recv()
                for step in range(1, heads):
                    forward(step, c).start()
            if c > 0:
                for step in range(1, heads):
                    forward(step, c - 1).wait_recv()

        pieces = []
        for step in range(heads):
            at = c if step == 0 else c - 1
            if 0 <= at < chunks:
                owner = lax.rem(me + heads - step, heads)
                part = x2[owner, :, pl.ds(at * CHUNK, CHUNK)].astype(F32)
                squares += jnp.sum(part * part, axis=-1, keepdims=True)
                pieces.append((part, owner * width + at * CHUNK))
        if c == chunks:
            inverse2 = normalize(x2, squares, normed2)
            n2_copies = send_normed(normed2, 1)
        project(pieces, CHUNK, c == 0)
        if c == chunks - 2:
            handed1 = hand_on(n1_copies, 0)
        if c == chunks - 1:
            for copy in c1_copies + handed1:
                copy.wait_recv()
            grad[...] = grad_part(0)

    @pl.when(not_first)
    def _():
        value_copy.wait_recv()

    attend(lax.rem(section + sections, sections + 1), f2, att2, 1, inverse2)
    for c in range(chunks):
        own_tile(att2, c)
    for turn, copy in a_copies:
        if turn == 1:
            copy.wait_recv()
    for c in range(chunks):
        if c == chunks // 2:
            handed2 = hand_on(n2_copies, 1)
        out2[:, pl.ds(c * CHUNK, CHUNK)] = whole_tile(att2, x2, c)
    out2_store = local(out2, out2_hbm.at[0], out_sem.at[1])

    for copy in c2_copies + handed2:
        copy.wait_recv()
    grad[...] += grad_part(1)
    grad_store = local(grad, grad_hbm.at[0], out_sem.at[2])

    for copy in x_copies + c1_copies + c2_copies + n1_copies + n2_copies + handed1 + handed2:
        copy.wait_send()
    for _, copy in a_copies:
        copy.wait_send()

    @pl.when(not_last)
    def _():
        value_copy.wait_send()
        for c in range(chunks):
            z_copy(c).wait_send()

    @pl.when(not_first)
    def _():
        for c in range(chunks):
            for step in range(1, heads):
                forward(step, c).wait_send()

    out1_store.wait()
    out2_store.wait()
    grad_store.wait()


def store_kernel(*refs):
    sources, targets, buffers, load_sem, store_sem = refs[:3], refs[3:6], refs[6:9], refs[9], refs[10]
    loads, stores = [], []
    for source, target, buffer in zip(sources, targets, buffers):
        rows = source.shape[1] // STORE_BLOCKS
        for i in range(STORE_BLOCKS):
            block, n = pl.ds(i * rows, rows), len(loads)
            loads.append(
                pltpu.make_async_copy(source.at[0, block], buffer.at[block], load_sem.at[n])
            )
            stores.append(
                pltpu.make_async_copy(buffer.at[block], target.at[0, block], store_sem.at[n])
            )
    for load in loads:
        load.start()
    for load, store in zip(loads, stores):
        load.wait()
        store.start()
    for store in stores:
        store.wait()


def solution(mesh):
    sections, replicas, heads = (mesh.shape[a] for a in ("section", "dp", "head"))

    def per_device(
        segments,
        stream,
        entering,
        pending,
        gain,
        wq,
        wk,
        wv,
        wo,
        scale,
        blend,
        cotangent,
    ):
        _, tokens, width = stream.shape
        model = width * heads
        q_width, kv_width = wq.shape[2], wk.shape[2]
        grad_rows = model // replicas
        chunks = width // CHUNK
        others = heads - 1
        peers = replicas - 1
        dma = pltpu.SemaphoreType.DMA
        scratch = [
            pltpu.VMEM(segments.shape, jnp.int32),
            pltpu.VMEM(gain.shape, F32),
            pltpu.VMEM(scale.shape, F32),
            pltpu.VMEM(blend.shape, F32),
            pltpu.VMEM((model, q_width), BF16),
            pltpu.VMEM((model, kv_width), BF16),
            pltpu.VMEM((model, kv_width), BF16),
            pltpu.VMEM((model, width), BF16),
            pltpu.VMEM((heads, tokens, width), BF16),
            pltpu.VMEM((heads, tokens, width), BF16),
            pltpu.VMEM((tokens, kv_width), BF16),
            pltpu.VMEM((tokens, kv_width), BF16),
            pltpu.VMEM((tokens, model), BF16),
            pltpu.VMEM((tokens, model), BF16),
            pltpu.VMEM((tokens, q_width + 2 * kv_width), F32),
            pltpu.VMEM((heads, tokens, q_width), BF16),
            pltpu.VMEM((heads, tokens, q_width), BF16),
            pltpu.VMEM((tokens, width), BF16),
            pltpu.VMEM((tokens, width), BF16),
            pltpu.VMEM((tokens, width), F32),
            pltpu.VMEM((2, replicas, tokens, grad_rows), BF16),
            pltpu.VMEM((replicas, 2, tokens, kv_width), BF16),
            pltpu.VMEM((grad_rows, kv_width), F32),
            dma((7,)),
            dma((4 * heads + 4,)),
            dma((heads,)),
            dma((3,)),
            dma((others,)),
            dma((others,)),
            dma((2, peers)),
            dma((2, peers)),
            dma((2, peers)),
            dma((2, peers)),
            dma((2, others)),
            dma((2, others)),
            dma((chunks,)),
            dma((chunks,)),
            dma((others, chunks)),
            dma((others, chunks)),
            dma((1,)),
            dma((1,)),
            dma((2, peers, others)),
            dma((2, peers, others)),
        ]
        results = pl.pallas_call(
            functools.partial(kernel, sections, replicas, heads),
            out_shape=(
                jax.ShapeDtypeStruct(stream.shape, BF16),
                jax.ShapeDtypeStruct(stream.shape, BF16),
                jax.ShapeDtypeStruct((1, grad_rows, kv_width), F32),
            ),
            in_specs=[pl.BlockSpec(memory_space=pl.ANY)] * 12,
            out_specs=(pl.BlockSpec(memory_space=pl.ANY),) * 3,
            scratch_shapes=scratch,
            compiler_params=pltpu.CompilerParams(
                collective_id=0, has_side_effects=True, vmem_limit_bytes=56 * 1024 * 1024
            ),
        )(
            segments,
            stream,
            entering,
            pending,
            gain,
            wq,
            wk,
            wv,
            wo,
            scale,
            blend,
            cotangent,
        )
        return pl.pallas_call(
            store_kernel,
            out_shape=tuple(jax.ShapeDtypeStruct(r.shape, r.dtype) for r in results),
            in_specs=[pl.BlockSpec(memory_space=pl.ANY)] * 3,
            out_specs=(pl.BlockSpec(memory_space=pl.ANY),) * 3,
            scratch_shapes=[pltpu.VMEM(r.shape[1:], r.dtype) for r in results]
            + [dma((3 * STORE_BLOCKS,)), dma((3 * STORE_BLOCKS,))],
            compiler_params=pltpu.CompilerParams(vmem_limit_bytes=56 * 1024 * 1024),
        )(*results)

    return jax.shard_map(
        per_device,
        mesh=mesh,
        in_specs=(
            P(None, "dp"),
            P("section", "dp", "head"),
            P("dp", None),
            P("section", "dp", "head"),
            P("section", None),
            P("section", None, "head"),
            P("section", None, "head"),
            P("section", None, "head"),
            P("section", None, "head"),
            P("section", "head"),
            P("section", "head"),
            P("section", None, "dp", "head"),
        ),
        out_specs=(
            P("section", "dp", "head"),
            P("section", "dp", "head"),
            P("section", "dp", "head"),
        ),
        check_vma=False,
    )
```
